32 devices in a mesh: groups: 2 (over y), fsdp: 4 (over z), tp: 2 (over x), sub: 2 (over core).
Axes of the slice: x: 2, y: 2, z: 4, core: 2. Of those that a mesh axis runs over, the one named last changes fastest.
Arguments:
- inputs: bfloat16 [64, 4, 8192], P(('groups', 'fsdp', 'sub'), None, 'tp'), parts along dimension 0, may hold values from -6 to 6
- queries: bfloat16 [64, 4, 4096], P(('groups', 'fsdp', 'sub'), None, 'tp'), parts along dimension 0, may hold values from -40 to 40
- kv_cache: bfloat16 [2, 64, 256, 512], P(None, ('groups', 'fsdp', 'sub'), None, 'tp'), parts along dimension 1, may hold values from -4 to 4
- lengths: int32 [64], P(('groups', 'fsdp', 'sub')), parts along dimension 0, may hold values from 32 to 256, as said below
- base: bfloat16 [2, 8192, 512], P(None, None, 'tp'), may hold values from -0.0625 to 0.0625
- a_factor: bfloat16 [2, 256, 8192], P(None, 'tp', ('fsdp', 'sub')), may hold values from -0.0625 to 0.0625
- b_factor: bfloat16 [2, 512, 256], P(None, 'tp', ('fsdp', 'sub')), may hold values from -0.375 to 0.375
Outputs:
- fresh_kv: bfloat16 [2, 64, 4, 512], P(None, ('groups', 'fsdp', 'sub'), None, 'tp'), parts along dimension 1
- attended: bfloat16 [64, 4, 4096], P(('groups', 'fsdp', 'sub'), None, 'tp'), parts along dimension 0
The draws below stay inside these ranges and needn't reach their ends.
There are 2 independent parts, one for each index of `groups`. The reference program is written for one: setup_inputs(seed, part) draws one part's arguments, and reference() takes and returns one part's arrays. A program takes and returns all parts, laid end to end along the dimension named above; an argument that names none is the same for every part. Nothing has to cross between parts.
Inputs may be any that keep to these rules, and one draw needn't show every extreme that they name: `lengths`: some row in every draw has exactly 256.
All inputs are finite; a program needn't handle non-finite values.
Results may differ from the reference program's by a relative error of at most 0.0055.
Values may be sent and summed in bfloat16 or wider, within the bound.
No kernel may reach another device: no remote copies, remote signals or barrier semaphores. Data moves between devices by JAX's collectives and lax.ppermute only.
A program may use at most 64 MiB of HBM per device.

```python
import jax
import jax.numpy as jnp

D = 8192
HD = 128
R = 256
KVH = 4
STEPS = 4
CACHE = 256
QH = 32
KVC = 512
ROWS = 32


def cache_keys(key):
    shape = (ROWS, CACHE, KVH * HD)
    rough = jnp.clip(jax.random.normal(key, shape, jnp.float32), -4.0, 4.0)
    keys = rough
    second = keys[:, 1, :]
    return keys.at[:, 1, :].set(second)


def draw_kv_cache(key, part):
    keys = cache_keys(key)
    key = jax.random.fold_in(key, 5)
    values = jnp.clip(jax.random.normal(key, (ROWS, CACHE, KVH * HD), jnp.float32), -4.0, 4.0)
    return jnp.stack([keys, values]).astype(jnp.bfloat16)


def draw_queries(key, part):
    key = jax.random.fold_in(key, 9)
    result = jnp.clip(jax.random.normal(key, (ROWS, STEPS, QH * HD), jnp.float32), -4.0, 4.0)
    return result.astype(jnp.bfloat16)


def draw_lengths(key, part):
    key = jax.random.fold_in(key, 3)
    filled = jax.random.randint(jax.random.fold_in(key, 1), (ROWS,), CACHE // 8, CACHE + 1)
    longest = jax.random.randint(jax.random.fold_in(key, 2), (), 0, ROWS)
    return filled.at[longest].set(CACHE).astype(jnp.int32)


def level_of(rng, extent, pieces, smallest, top_value):
    loudness = 1.0
    for axis_at, shards_of in pieces:
        heights = jax.random.uniform(jax.random.fold_in(jax.random.fold_in(rng, 6), axis_at), (shards_of,), jnp.float32, smallest / len(pieces), top_value / len(pieces))
        loudness = loudness * jnp.repeat(jnp.exp(heights), extent[axis_at] // shards_of).reshape((-1,) + (1,) * (len(extent) - 1 - axis_at))
    return loudness


def centred(key, shape, width, reach, cuts=(), kind=jnp.bfloat16):
    entries = jax.random.normal(key, shape, jnp.float32) * width
    if len(cuts) > 0:
        entries = level_of(key, shape, cuts, -0.22, 0.18) * entries
    return jnp.clip(entries, min=-reach, max=reach).astype(kind)


def setup_inputs(seed: int = 0, part: int = 0) -> dict:
    key_list = jax.random.split(jax.random.key(seed), 8)
    own_keys = jax.random.split(jax.random.fold_in(key_list[7], part), 8)
    inputs = centred(own_keys[0], (ROWS, STEPS, D), 1.0, 6.0, ((0, 8), (2, 2)))
    queries = draw_queries(jax.random.fold_in(jax.random.fold_in(key_list[7], part), 71), part)
    kv_cache = draw_kv_cache(jax.random.fold_in(jax.random.fold_in(key_list[7], part), 71), part)
    lengths = draw_lengths(jax.random.fold_in(jax.random.fold_in(key_list[7], part), 71), part)
    base = centred(key_list[4], (2, D, KVC), D ** -0.5, 0.0625, ((2, 2),))
    a_factor = centred(key_list[5], (2, R, D), D ** -0.5, 0.0625, ((1, 2), (2, 8)))
    b_factor = centred(key_list[6], (2, KVC, R), R ** -0.5, 0.375, ((1, 2), (2, 8)))
    return {"inputs": inputs, "queries": queries, "kv_cache": kv_cache, "lengths": lengths, "base": base, "a_factor": a_factor, "b_factor": b_factor}


def attend(queries, kv_cache, fresh, lengths):
    rows, steps = queries.shape[0], queries.shape[1]
    heads_kv = fresh.shape[3] // HD
    group = QH // KVH
    cached = kv_cache.shape[2]
    scale = HD ** -0.5
    query = queries.astype(jnp.float32).reshape(rows, steps, heads_kv, group, HD)
    keys_old = kv_cache[0].astype(jnp.float32).reshape(rows, cached, heads_kv, HD)
    values_old = kv_cache[1].astype(jnp.float32).reshape(rows, cached, heads_kv, HD)
    keys_new = fresh[0].astype(jnp.float32).reshape(rows, steps, heads_kv, HD)
    values_new = fresh[1].astype(jnp.float32).reshape(rows, steps, heads_kv, HD)
    old_scores = jnp.einsum("bskgh,blkh->bkgsl", query, keys_old) * scale
    new_scores = jnp.einsum("bskgh,bukh->bkgsu", query, keys_new) * scale
    positions = jnp.arange(cached, dtype=jnp.int32)
    valid_old = (positions[None, :] < lengths[:, None])[:, None, None, None, :]
    order = jnp.arange(steps, dtype=jnp.int32)
    valid_new = (order[None, :] <= order[:, None])[None, None, None, :, :]
    old_scores = jnp.where(valid_old, old_scores, -jnp.inf)
    new_scores = jnp.where(valid_new, new_scores, -jnp.inf)
    top = jnp.maximum(jnp.max(old_scores, axis=-1), jnp.max(new_scores, axis=-1))
    old_exp = jnp.where(valid_old, jnp.exp(old_scores - top[..., None]), 0.0)
    new_exp = jnp.where(valid_new, jnp.exp(new_scores - top[..., None]), 0.0)
    total = jnp.sum(old_exp, axis=-1) + jnp.sum(new_exp, axis=-1)
    old_weights = (old_exp / total[..., None]).astype(jnp.bfloat16).astype(jnp.float32)
    new_weights = (new_exp / total[..., None]).astype(jnp.bfloat16).astype(jnp.float32)
    mixed = jnp.einsum("bkgsl,blkh->bskgh", old_weights, values_old)
    mixed = mixed + jnp.einsum("bkgsu,bukh->bskgh", new_weights, values_new)
    return mixed.astype(jnp.bfloat16).reshape(rows, steps, heads_kv * group * HD)


def reference(inputs, queries, kv_cache, lengths, base, a_factor, b_factor):
    merged_list = []
    for which in range(2):
        delta = jnp.dot(a_factor[which].T, b_factor[which].T, preferred_element_type=jnp.float32)
        merged_list.append((base[which].astype(jnp.float32) + delta).astype(jnp.bfloat16))
    flat_inputs = inputs.reshape(ROWS * STEPS, D)
    fresh_list = []
    for which in range(2):
        fresh_list.append(jnp.dot(flat_inputs, merged_list[which], preferred_element_type=jnp.float32))
    fresh = jnp.stack(fresh_list).astype(jnp.bfloat16).reshape(2, ROWS, STEPS, KVC)
    attended = attend(queries, kv_cache, fresh, lengths)
    return fresh, attended
```

```python
import functools

import jax
import jax.numpy as jnp
from jax import lax
from jax.experimental import pallas as pl
from jax.experimental.pallas import tpu as pltpu
from jax.sharding import PartitionSpec as P

HD = 128
KVH = 4
QH = 32
NEG = -1e30
VMEM_LIMIT = 40 * 2**20

NT = (((1,), (1,)), ((), ()))
NN = (((1,), (0,)), ((), ()))


def dot(x, y, dims=NN):
    return lax.dot_general(x, y, dims, preferred_element_type=jnp.float32)


def vmem():
    return pl.BlockSpec(memory_space=pltpu.VMEM)


def params():
    return pltpu.CompilerParams(vmem_limit_bytes=VMEM_LIMIT)


def cache_kernel(group, len_ref, q_ref, kv_ref, q_out, acc_out, top_out, sum_out):
    rows, steps, width = q_ref.shape
    heads, cached = width // (group * HD), kv_ref.shape[2]
    tokens = rows * steps
    flat = jnp.concatenate([q_ref[b].astype(jnp.float32) for b in range(rows)], axis=0)
    flat = flat.astype(jnp.bfloat16)
    count = group * tokens
    row_of = (lax.broadcasted_iota(jnp.int32, (count, 1), 0) % tokens) // steps
    filled = jnp.zeros((count, 1), jnp.int32)
    for b in range(rows):
        filled = jnp.where(row_of == b, len_ref[b], filled)
    position = lax.broadcasted_iota(jnp.int32, (count, cached), 1)
    for g in range(heads):
        query = jnp.concatenate(
            [flat[:, (g * group + h) * HD : (g * group + h + 1) * HD] for h in range(group)], axis=0
        )
        q_out[g] = query
        cols = slice(g * HD, (g + 1) * HD)
        scores = []
        for b in range(rows):
            valid = jnp.logical_and(row_of == b, position < filled)
            scores.append(jnp.where(valid, dot(query, kv_ref[0, b, :, cols], NT) * HD**-0.5, NEG))
        top = functools.reduce(jnp.maximum, [jnp.max(x, axis=1, keepdims=True) for x in scores])
        total = jnp.zeros((count, 1), jnp.float32)
        mixed = jnp.zeros((count, HD), jnp.float32)
        for b in range(rows):
            weight = jnp.exp(scores[b] - top)
            total = total + jnp.sum(weight, axis=1, keepdims=True)
            high = weight.astype(jnp.bfloat16)
            low = (weight - high.astype(jnp.float32)).astype(jnp.bfloat16)
            values = kv_ref[1, b, :, cols]
            mixed = mixed + dot(high, values) + dot(low, values)
        acc_out[g] = mixed
        top_out[g] = jnp.broadcast_to(top, (count, HD))
        sum_out[g] = jnp.broadcast_to(total, (count, HD))


def early_kernel(blocks, place_ref, base_ref, *refs):
    x_refs, a_refs, out_ref = refs[:blocks], refs[blocks:-1], refs[-1]
    step, width, columns = pl.program_id(0), base_ref.shape[1], base_ref.shape[2]
    tokens, slab, ranks = x_refs[0].shape[0], a_refs[0].shape[2], a_refs[0].shape[1]

    def stacked(start, size):
        return jnp.concatenate([x[:, pl.ds(start, size)] for x in x_refs], axis=0)

    @pl.when(step == 0)
    def _():
        for m in range(2):
            total = jnp.zeros((blocks * tokens, ranks), jnp.float32)
            for i, a in enumerate(a_refs):
                start = pl.multiple_of(place_ref[1 + i] * slab, slab)
                total = total + dot(stacked(start, slab), a[m], NT)
            out_ref[:, 2 * columns + m * ranks : 2 * columns + (m + 1) * ranks] = total
        out_ref[:, : 2 * columns] = jnp.zeros((blocks * tokens, 2 * columns), jnp.float32)

    x = stacked(pl.multiple_of(step * width, width), width)
    for m in range(2):
        cols = slice(m * columns, (m + 1) * columns)
        out_ref[:, cols] = out_ref[:, cols] + dot(x, base_ref[m])


def late_kernel(blocks, columns, place_ref, part_ref, *refs):
    x_refs, outs = refs[:blocks], refs[-blocks:]
    a_refs = refs[blocks:-blocks]
    tokens, slab, ranks = x_refs[0].shape[0], a_refs[0].shape[2], a_refs[0].shape[1]
    acc = part_ref.shape[1]
    sums = [part_ref[:, : 2 * columns]]
    for m in range(2):
        total = part_ref[:, 2 * columns + m * ranks : 2 * columns + (m + 1) * ranks]
        for i, a in enumerate(a_refs):
            start = pl.multiple_of(place_ref[i] * slab, slab)
            x = jnp.concatenate([x[:, pl.ds(start, slab)] for x in x_refs], axis=0)
            total = total + dot(x, a[m], NT)
        sums.append(total)
    whole = jnp.concatenate(sums, axis=1)
    shift = place_ref[len(a_refs)]
    for j, out in enumerate(outs):
        value = jnp.zeros((tokens, acc), jnp.float32)
        for k in range(blocks):
            mine = lax.rem(shift - k + blocks, blocks) == j
            value = jnp.where(mine, whole[k * tokens : (k + 1) * tokens], value)
        out[...] = value.astype(out.dtype)


def rank_kernel(columns, mine_ref, *refs):
    total = mine_ref[:, 2 * columns :]
    for other in refs[:-1]:
        total = total + other[:, 2 * columns :].astype(jnp.float32)
    refs[-1][...] = total.astype(jnp.bfloat16)


def final_kernel(blocks, steps, group, place_ref, mine_ref, *refs):
    others, refs = refs[: blocks - 1], refs[blocks - 1 :]
    rank_refs, refs = refs[:blocks], refs[blocks:]
    up_ref, q_ref, acc_ref, top_ref, sum_ref, fresh_out, out = refs
    tokens, columns = mine_ref.shape[0], fresh_out.shape[3]
    rows, heads = tokens // steps, columns // HD
    ranks = rank_refs[0].shape[1] // 2
    fresh = []
    for m in range(2):
        cols = slice(m * columns, (m + 1) * columns)
        total = mine_ref[:, cols]
        for other in others:
            total = total + other[:, cols].astype(jnp.float32)
        for i, rank in enumerate(rank_refs):
            start = pl.multiple_of(place_ref[i] * ranks, ranks)
            total = total + dot(rank[:, m * ranks : (m + 1) * ranks], up_ref[m, pl.ds(start, ranks)])
        for b in range(rows):
            fresh_out[m, b] = total[b * steps : (b + 1) * steps].astype(jnp.bfloat16)
        fresh.append(total.astype(jnp.bfloat16))
    count = group * tokens
    token = lax.broadcasted_iota(jnp.int32, (count, tokens), 0) % tokens
    key = lax.broadcasted_iota(jnp.int32, (count, tokens), 1)
    valid = jnp.logical_and(token // steps == key // steps, key <= token)
    for g in range(heads):
        cols = slice(g * HD, (g + 1) * HD)
        scores = jnp.where(valid, dot(q_ref[g], fresh[0][:, cols], NT) * HD**-0.5, NEG)
        top_old = top_ref[g][:, :1]
        top = jnp.maximum(top_old, jnp.max(scores, axis=1, keepdims=True))
        scale = jnp.exp(top_old - top)
        weight = jnp.where(valid, jnp.exp(scores - top), 0.0)
        total = sum_ref[g][:, :1] * scale + jnp.sum(weight, axis=1, keepdims=True)
        weight = (weight / total).astype(jnp.bfloat16)
        mixed = acc_ref[g] * (scale / total) + dot(weight, fresh[1][:, cols])
        for h in range(group):
            lanes = slice((g * group + h) * HD, (g * group + h + 1) * HD)
            for b in range(rows):
                at = h * tokens + b * steps
                out[b, :, lanes] = mixed[at : at + steps].astype(jnp.bfloat16)


def smem():
    return pl.BlockSpec(memory_space=pltpu.SMEM)


def local(sizes, inputs, queries, kv_cache, lengths, base, a_factor, b_factor):
    fsdp, tp, sub = sizes
    inner = fsdp // tp
    row_count, steps, wide = inputs.shape
    tokens, columns, ranks = row_count * steps, base.shape[2], a_factor.shape[1]
    heads, group = columns // HD, QH // KVH
    f, t, s = lax.axis_index("fsdp"), lax.axis_index("tp"), lax.axis_index("sub")
    p, r = f // inner, f % inner
    bf16, f32 = jnp.bfloat16, jnp.float32

    def over_fsdp(x, k):
        return lax.ppermute(x, "fsdp", [(i, i ^ k) for i in range(fsdp)])

    def over_sub(x, k):
        return lax.ppermute(x, "sub", [(i, i ^ k) for i in range(sub)])

    slabs = [(0, 0, a_factor)]
    for k in range(1, inner):
        slabs.append((k, 0, over_fsdp(a_factor, k)))
    slabs = slabs + [(k, e, over_sub(a, e)) for k, _, a in slabs for e in range(1, sub)]
    early = [x for x in slabs if x[0] == 0]
    late = [x for x in slabs if x[0] != 0]

    x = inputs.reshape(tokens, wide)
    xs = []
    for k in range(tp):
        pairs = []
        for i in range(fsdp):
            for j in range(tp):
                pairs.append((i * tp + j, (j * inner + i % inner) * tp + (i // inner + k) % tp))
        xs.append(lax.ppermute(x, ("fsdp", "tp"), pairs))

    up = b_factor.transpose(0, 2, 1)[:, None]

    def join(mine, other, bit):
        low = jnp.where(bit == 0, mine, other)
        high = jnp.where(bit == 0, other, mine)
        return jnp.concatenate([low, high], axis=1)

    for axis, size, index in (("sub", sub, s), ("fsdp", fsdp, f)):
        k = 1
        while k < size:
            other = lax.ppermute(up, axis, [(i, i ^ k) for i in range(size)])
            up = join(up, other, (index // k) % 2)
            k = k * 2
    up = up.reshape(2, -1, columns)

    count = group * tokens
    per_head = jax.ShapeDtypeStruct((heads, count, HD), f32)
    query, mixed, top, total = pl.pallas_call(
        functools.partial(cache_kernel, group),
        out_shape=(jax.ShapeDtypeStruct((heads, count, HD), bf16), per_head, per_head, per_head),
        in_specs=[smem(), vmem(), vmem()],
        out_specs=[vmem()] * 4,
        compiler_params=params(),
        name="cached",
    )(lengths, queries, kv_cache)

    def place_of(items):
        return [((r ^ k) * sub + (s ^ e)).astype(jnp.int32) for k, e, _ in items]

    width = 2 * columns + 2 * ranks
    chunk = wide // 4
    part = pl.pallas_call(
        functools.partial(early_kernel, tp),
        out_shape=jax.ShapeDtypeStruct((tp * tokens, width), f32),
        grid_spec=pltpu.PrefetchScalarGridSpec(
            num_scalar_prefetch=1,
            grid=(wide // chunk,),
            in_specs=[
                pl.BlockSpec((2, chunk, columns), lambda i, at: (0, at[0] * (wide // chunk) + i, 0))
            ]
            + [vmem()] * (tp + len(early)),
            out_specs=vmem(),
        ),
        compiler_params=params(),
        name="early",
    )(jnp.stack([p.astype(jnp.int32)] + place_of(early)), base, *xs, *[a for _, _, a in early])

    shift = ((t - p + tp) % tp).astype(jnp.int32)
    parts = pl.pallas_call(
        functools.partial(late_kernel, tp, columns),
        out_shape=[jax.ShapeDtypeStruct((tokens, width), f32 if j == 0 else bf16) for j in range(tp)],
        in_specs=[smem()] + [vmem()] * (1 + tp + len(late)),
        out_specs=[vmem()] * tp,
        compiler_params=params(),
        name="late",
    )(jnp.stack(place_of(late) + [shift]), part, *xs, *[a for _, _, a in late])

    others = []
    for j in range(1, tp):
        pairs = [(i, (i + j * inner) % fsdp) for i in range(fsdp)]
        others.append(lax.ppermute(parts[j], "fsdp", pairs))
    own = pl.pallas_call(
        functools.partial(rank_kernel, columns),
        out_shape=jax.ShapeDtypeStruct((tokens, 2 * ranks), bf16),
        in_specs=[vmem()] * tp,
        out_specs=vmem(),
        compiler_params=params(),
        name="ranks",
    )(parts[0], *others)
    rank_parts = [own]
    for i in range(1, tp):
        rank_parts.append(lax.ppermute(own, "tp", [(j, (j + i) % tp) for j in range(tp)]))
    rank_place = jnp.stack([((t - i + tp) % tp).astype(jnp.int32) for i in range(tp)])

    fresh, attended = pl.pallas_call(
        functools.partial(final_kernel, tp, steps, group),
        out_shape=(
            jax.ShapeDtypeStruct((2, row_count, steps, columns), bf16),
            jax.ShapeDtypeStruct(queries.shape, bf16),
        ),
        in_specs=[smem()] + [vmem()] * (2 * tp + 5),
        out_specs=[vmem(), vmem()],
        compiler_params=params(),
        name="final",
    )(rank_place, parts[0], *others, *rank_parts, up, query, mixed, top, total)
    return fresh, attended


def solution(mesh):
    sizes = tuple(mesh.shape[axis] for axis in ("fsdp", "tp", "sub"))
    return jax.shard_map(
        functools.partial(local, sizes),
        mesh=mesh,
        in_specs=(
            P(("groups", "fsdp", "sub"), None, "tp"),
            P(("groups", "fsdp", "sub"), None, "tp"),
            P(None, ("groups", "fsdp", "sub"), None, "tp"),
            P(("groups", "fsdp", "sub")),
            P(None, None, "tp"),
            P(None, "tp", ("fsdp", "sub")),
            P(None, "tp", ("fsdp", "sub")),
        ),
        out_specs=(
            P(None, ("groups", "fsdp", "sub"), None, "tp"),
            P(("groups", "fsdp", "sub"), None, "tp"),
        ),
        check_vma=False,
    )
```

```python
import functools

import jax
import jax.numpy as jnp
from jax import lax
from jax.experimental import pallas as pl
from jax.experimental.pallas import tpu as pltpu
from jax.sharding import PartitionSpec as P

HD = 128
KVH = 4
QH = 32
NEG = -1e30

NT = (((1,), (1,)), ((), ()))
NN = (((1,), (0,)), ((), ()))


def dot(x, y, dims=NN):
    return lax.dot_general(x, y, dims, preferred_element_type=jnp.float32)


def vmem():
    return pl.BlockSpec(memory_space=pltpu.VMEM)


def params(mib=40):
    return pltpu.CompilerParams(vmem_limit_bytes=mib * 2**20)


def cache_kernel(
    group, len_ref, place_ref, q_hbm, kv_hbm, base_hbm, a_hbm,
    q_out, acc_out, top_out, sum_out, base_out, a_out, q_ref, kv_ref, sems,
):
    wide = base_out.shape[1]
    start = pl.multiple_of(place_ref[0] * wide, wide)
    copies = [
        pltpu.make_async_copy(q_hbm, q_ref, sems.at[0]),
        pltpu.make_async_copy(kv_hbm.at[0], kv_ref.at[0], sems.at[1]),
        pltpu.make_async_copy(kv_hbm.at[1], kv_ref.at[1], sems.at[2]),
        pltpu.make_async_copy(a_hbm, a_out, sems.at[3]),
        pltpu.make_async_copy(base_hbm.at[0, pl.ds(start, wide)], base_out.at[0], sems.at[4]),
        pltpu.make_async_copy(base_hbm.at[1, pl.ds(start, wide)], base_out.at[1], sems.at[5]),
    ]
    for copy in copies:
        copy.start()
    for copy in copies[:3]:
        copy.wait()
    rows, steps, width = q_ref.shape
    heads, cached = width // (group * HD), kv_ref.shape[2]
    tokens = rows * steps
    flat = jnp.concatenate([q_ref[b].astype(jnp.float32) for b in range(rows)], axis=0)
    flat = flat.astype(jnp.bfloat16)
    count = group * tokens
    row_of = (lax.broadcasted_iota(jnp.int32, (count, 1), 0) % tokens) // steps
    filled = jnp.zeros((count, 1), jnp.int32)
    for b in range(rows):
        filled = jnp.where(row_of == b, len_ref[b], filled)
    position = lax.broadcasted_iota(jnp.int32, (count, cached), 1)
    for g in range(heads):
        query = jnp.concatenate(
            [flat[:, (g * group + h) * HD : (g * group + h + 1) * HD] for h in range(group)], axis=0
        )
        q_out[g] = query
        cols = slice(g * HD, (g + 1) * HD)
        scores = []
        for b in range(rows):
            valid = jnp.logical_and(row_of == b, position < filled)
            scores.append(jnp.where(valid, dot(query, kv_ref[0, b, :, cols], NT) * HD**-0.5, NEG))
        top = functools.reduce(jnp.maximum, [jnp.max(x, axis=1, keepdims=True) for x in scores])
        total = jnp.zeros((count, 1), jnp.float32)
        mixed = jnp.zeros((count, HD), jnp.float32)
        for b in range(rows):
            weight = jnp.exp(scores[b] - top)
            total = total + jnp.sum(weight, axis=1, keepdims=True)
            high = weight.astype(jnp.bfloat16)
            low = (weight - high.astype(jnp.float32)).astype(jnp.bfloat16)
            values = kv_ref[1, b, :, cols]
            mixed = mixed + dot(high, values) + dot(low, values)
        acc_out[g] = mixed
        top_out[g] = jnp.broadcast_to(top, (count, HD))
        sum_out[g] = jnp.broadcast_to(total, (count, HD))
    for copy in copies[3:]:
        copy.wait()


def early_kernel(blocks, place_ref, base_ref, *refs):
    x_refs, a_refs = refs[:blocks], refs[blocks:-2]
    out_ref, x_out = refs[-2:]
    columns, slab, ranks = base_ref.shape[2], a_refs[0].shape[2], a_refs[0].shape[1]
    rows, steps, wide = x_refs[0].shape
    for k, x_ref in enumerate(x_refs):
        x = jnp.concatenate([x_ref[b].astype(jnp.float32) for b in range(rows)], axis=0)
        x_out[k * rows * steps : (k + 1) * rows * steps] = x.astype(jnp.bfloat16)
    count = blocks * rows * steps
    for m in range(2):
        out_ref[:, m * columns : (m + 1) * columns] = dot(x_out[...], base_ref[m])
        total = jnp.zeros((count, ranks), jnp.float32)
        for i, a in enumerate(a_refs):
            start = pl.multiple_of(place_ref[i] * slab, slab)
            total = total + dot(x_out[:, pl.ds(start, slab)], a[m], NT)
        out_ref[:, 2 * columns + m * ranks : 2 * columns + (m + 1) * ranks] = total


def late_kernel(blocks, columns, place_ref, part_ref, x_ref, *refs):
    a_refs, outs = refs[:-blocks], refs[-blocks:]
    tokens, acc = outs[0].shape
    slab, ranks = a_refs[0].shape[2], a_refs[0].shape[1]
    sums = [part_ref[:, : 2 * columns]]
    for m in range(2):
        total = part_ref[:, 2 * columns + m * ranks : 2 * columns + (m + 1) * ranks]
        for i, a in enumerate(a_refs):
            start = pl.multiple_of(place_ref[i] * slab, slab)
            total = total + dot(x_ref[:, pl.ds(start, slab)], a[m], NT)
        sums.append(total)
    whole = jnp.concatenate(sums, axis=1)
    shift = place_ref[len(a_refs)]
    for j, out in enumerate(outs):
        value = jnp.zeros((tokens, acc), jnp.float32)
        for k in range(blocks):
            mine = lax.rem(shift - k + blocks, blocks) == j
            value = jnp.where(mine, whole[k * tokens : (k + 1) * tokens], value)
        out[...] = value.astype(out.dtype)


def rank_kernel(columns, mine_ref, *refs):
    total = mine_ref[:, 2 * columns :]
    for other in refs[:-1]:
        total = total + other[:, 2 * columns :].astype(jnp.float32)
    refs[-1][...] = total.astype(jnp.bfloat16)


def final_kernel(blocks, steps, group, place_ref, mine_ref, *refs):
    others, refs = refs[: blocks - 1], refs[blocks - 1 :]
    rank_refs, refs = refs[:blocks], refs[blocks:]
    up_ref, q_ref, acc_ref, top_ref, sum_ref, fresh_out, out = refs
    tokens, columns = mine_ref.shape[0], fresh_out.shape[3]
    rows, heads = tokens // steps, columns // HD
    ranks = rank_refs[0].shape[1] // 2
    fresh = []
    for m in range(2):
        cols = slice(m * columns, (m + 1) * columns)
        total = mine_ref[:, cols]
        for other in others:
            total = total + other[:, cols].astype(jnp.float32)
        for i, rank in enumerate(rank_refs):
            start = pl.multiple_of(place_ref[i] * ranks, ranks)
            total = total + dot(rank[:, m * ranks : (m + 1) * ranks], up_ref[m, pl.ds(start, ranks)])
        for b in range(rows):
            fresh_out[m, b] = total[b * steps : (b + 1) * steps].astype(jnp.bfloat16)
        fresh.append(total.astype(jnp.bfloat16))
    count = group * tokens
    token = lax.broadcasted_iota(jnp.int32, (count, tokens), 0) % tokens
    key = lax.broadcasted_iota(jnp.int32, (count, tokens), 1)
    valid = jnp.logical_and(token // steps == key // steps, key <= token)
    for g in range(heads):
        cols = slice(g * HD, (g + 1) * HD)
        scores = jnp.where(valid, dot(q_ref[g], fresh[0][:, cols], NT) * HD**-0.5, NEG)
        top_old = top_ref[g][:, :1]
        top = jnp.maximum(top_old, jnp.max(scores, axis=1, keepdims=True))
        scale = jnp.exp(top_old - top)
        weight = jnp.where(valid, jnp.exp(scores - top), 0.0)
        total = sum_ref[g][:, :1] * scale + jnp.sum(weight, axis=1, keepdims=True)
        weight = (weight / total).astype(jnp.bfloat16)
        mixed = acc_ref[g] * (scale / total) + dot(weight, fresh[1][:, cols])
        for h in range(group):
            lanes = slice((g * group + h) * HD, (g * group + h + 1) * HD)
            for b in range(rows):
                at = h * tokens + b * steps
                out[b, :, lanes] = mixed[at : at + steps].astype(jnp.bfloat16)


def smem():
    return pl.BlockSpec(memory_space=pltpu.SMEM)


def local(sizes, inputs, queries, kv_cache, lengths, base, a_factor, b_factor):
    fsdp, tp, sub = sizes
    inner = fsdp // tp
    row_count, steps, wide = inputs.shape
    tokens, columns, ranks = row_count * steps, base.shape[2], a_factor.shape[1]
    heads, group = columns // HD, QH // KVH
    f, t, s = lax.axis_index("fsdp"), lax.axis_index("tp"), lax.axis_index("sub")
    p, r = f // inner, f % inner
    bf16, f32 = jnp.bfloat16, jnp.float32

    def over_fsdp(x, k):
        return lax.ppermute(x, "fsdp", [(i, i ^ k) for i in range(fsdp)])

    def over_sub(x, k):
        return lax.ppermute(x, "sub", [(i, i ^ k) for i in range(sub)])

    def spread(x, k):
        pairs = []
        for i in range(fsdp):
            for j in range(tp):
                pairs.append((i * tp + j, (j * inner + i % inner) * tp + (i // inner + k) % tp))
        return lax.ppermute(x, ("fsdp", "tp"), pairs)

    xs = [None] + [spread(inputs, k) for k in range(1, tp)]
    far = [over_fsdp(a_factor, k) for k in range(1, inner)]
    near = [(0, e, over_sub(a_factor, e)) for e in range(1, sub)]
    xs[0] = spread(inputs, 0)

    def join(mine, other, bit):
        low = jnp.where(bit == 0, mine, other)
        high = jnp.where(bit == 0, other, mine)
        return jnp.concatenate([low, high], axis=1)

    def gather(x, axis, index, start, stop):
        size = {"fsdp": fsdp, "sub": sub}[axis]
        while start < stop:
            other = lax.ppermute(x, axis, [(i, i ^ start) for i in range(size)])
            x = join(x, other, (index // start) % 2)
            start = start * 2
        return x

    up = gather(b_factor.transpose(0, 2, 1)[:, None], "fsdp", f, 1, inner)

    count = group * tokens
    per_head = jax.ShapeDtypeStruct((heads, count, HD), f32)
    *state, rows_base, near_a = pl.pallas_call(
        functools.partial(cache_kernel, group),
        out_shape=[
            jax.ShapeDtypeStruct((heads, count, HD), bf16),
            per_head,
            per_head,
            per_head,
            jax.ShapeDtypeStruct((2, wide, columns), bf16),
            jax.ShapeDtypeStruct(a_factor.shape, bf16),
        ],
        in_specs=[smem(), smem()] + [pl.BlockSpec(memory_space=pltpu.HBM)] * 4,
        out_specs=[vmem()] * 6,
        scratch_shapes=[
            pltpu.VMEM(queries.shape, bf16),
            pltpu.VMEM(kv_cache.shape, bf16),
            pltpu.SemaphoreType.DMA((6,)),
        ],
        compiler_params=params(),
        name="cached",
    )(lengths, p.astype(jnp.int32)[None], queries, kv_cache, base, a_factor)

    def place_of(items):
        return [((r ^ k) * sub + (s ^ e)).astype(jnp.int32) for k, e, _ in items]

    xs, near_a = lax.optimization_barrier((xs, near_a))
    near = [(0, 0, near_a)] + near
    width = 2 * columns + 2 * ranks
    part, x = pl.pallas_call(
        functools.partial(early_kernel, tp),
        out_shape=[
            jax.ShapeDtypeStruct((tp * tokens, width), f32),
            jax.ShapeDtypeStruct((tp * tokens, wide), bf16),
        ],
        in_specs=[smem()] + [vmem()] * (1 + tp + len(near)),
        out_specs=[vmem()] * 2,
        compiler_params=params(),
        name="early",
    )(jnp.stack(place_of(near)), rows_base, *xs, *[a for _, _, a in near])

    far, part, up = lax.optimization_barrier((far, part, up))
    late = [(k, e, over_sub(a, e) if e else a) for k, a in enumerate(far, 1) for e in range(sub)]
    shift = ((t - p + tp) % tp).astype(jnp.int32)
    parts = pl.pallas_call(
        functools.partial(late_kernel, tp, columns),
        out_shape=[jax.ShapeDtypeStruct((tokens, width), f32 if j == 0 else bf16) for j in range(tp)],
        in_specs=[smem()] + [vmem()] * (2 + len(late)),
        out_specs=[vmem()] * tp,
        compiler_params=params(),
        name="late",
    )(jnp.stack(place_of(late) + [shift]), part, x, *[a for _, _, a in late])

    parts, up = lax.optimization_barrier((parts, up))
    others = []
    for j in range(1, tp):
        pairs = [(i, (i + j * inner) % fsdp) for i in range(fsdp)]
        others.append(lax.ppermute(parts[j], "fsdp", pairs))
    up = gather(up, "fsdp", f, inner, fsdp)
    own = pl.pallas_call(
        functools.partial(rank_kernel, columns),
        out_shape=jax.ShapeDtypeStruct((tokens, 2 * ranks), bf16),
        in_specs=[vmem()] * tp,
        out_specs=vmem(),
        compiler_params=params(),
        name="ranks",
    )(parts[0], *others)
    own, up = lax.optimization_barrier((own, up))
    up = gather(up, "sub", s, 1, sub)
    up = up.reshape(2, sub, fsdp, -1, columns).swapaxes(1, 2).reshape(2, -1, columns)
    rank_parts = [own]
    for i in range(1, tp):
        rank_parts.append(lax.ppermute(own, "tp", [(j, (j + i) % tp) for j in range(tp)]))
    rank_place = jnp.stack([((t - i + tp) % tp).astype(jnp.int32) for i in range(tp)])

    fresh, attended = pl.pallas_call(
        functools.partial(final_kernel, tp, steps, group),
        out_shape=(
            jax.ShapeDtypeStruct((2, row_count, steps, columns), bf16),
            jax.ShapeDtypeStruct(queries.shape, bf16),
        ),
        in_specs=[smem()] + [vmem()] * (2 * tp + 5),
        out_specs=[vmem(), vmem()],
        compiler_params=params(),
        name="final",
    )(rank_place, parts[0], *others, *rank_parts, up, *state)
    return fresh, attended


def solution(mesh):
    sizes = tuple(mesh.shape[axis] for axis in ("fsdp", "tp", "sub"))
    return jax.shard_map(
        functools.partial(local, sizes),
        mesh=mesh,
        in_specs=(
            P(("groups", "fsdp", "sub"), None, "tp"),
            P(("groups", "fsdp", "sub"), None, "tp"),
            P(None, ("groups", "fsdp", "sub"), None, "tp"),
            P(("groups", "fsdp", "sub")),
            P(None, None, "tp"),
            P(None, "tp", ("fsdp", "sub")),
            P(None, "tp", ("fsdp", "sub")),
        ),
        out_specs=(
            P(None, ("groups", "fsdp", "sub"), None, "tp"),
            P(("groups", "fsdp", "sub"), None, "tp"),
        ),
        check_vma=False,
    )
```

```python
import functools

import jax
import jax.numpy as jnp
from jax import lax
from jax.experimental import pallas as pl
from jax.experimental.pallas import tpu as pltpu
from jax.sharding import PartitionSpec as P

HD = 128
KVH = 4
QH = 32

C_CACHED = 4.0
C_EARLY = 0.1
NEG = -1e30

NT = (((1,), (1,)), ((), ()))
NN = (((1,), (0,)), ((), ()))


def dot(x, y, dims=NN):
    return lax.dot_general(x, y, dims, preferred_element_type=jnp.float32)


def cost(us):
    return pl.CostEstimate(flops=int(us * 1e9), bytes_accessed=int(us * 3e6), transcendentals=0)


def vmem():
    return pl.BlockSpec(memory_space=pltpu.VMEM)


def params(mib=40):
    return pltpu.CompilerParams(vmem_limit_bytes=mib * 2**20)


def cache_kernel(
    group, len_ref, q_hbm, kv_hbm, a_hbm,
    q_out, acc_out, top_out, sum_out, a_out, q_ref, kv_ref, sems,
):
    copies = [
        pltpu.make_async_copy(q_hbm, q_ref, sems.at[0]),
        pltpu.make_async_copy(kv_hbm.at[0], kv_ref.at[0], sems.at[1]),
        pltpu.make_async_copy(kv_hbm.at[1], kv_ref.at[1], sems.at[2]),
        pltpu.make_async_copy(a_hbm, a_out, sems.at[3]),
    ]
    for copy in copies:
        copy.start()
    for copy in copies[:3]:
        copy.wait()
    rows, steps, width = q_ref.shape
    heads, cached = width // (group * HD), kv_ref.shape[2]
    tokens = rows * steps
    flat = jnp.concatenate([q_ref[b].astype(jnp.float32) for b in range(rows)], axis=0)
    flat = flat.astype(jnp.bfloat16)
    count = group * tokens
    row_of = (lax.broadcasted_iota(jnp.int32, (count, 1), 0) % tokens) // steps
    filled = jnp.zeros((count, 1), jnp.int32)
    for b in range(rows):
        filled = jnp.where(row_of == b, len_ref[b], filled)
    position = lax.broadcasted_iota(jnp.int32, (count, cached), 1)
    for g in range(heads):
        query = jnp.concatenate(
            [flat[:, (g * group + h) * HD : (g * group + h + 1) * HD] for h in range(group)], axis=0
        )
        q_out[g] = query
        cols = slice(g * HD, (g + 1) * HD)
        scores = []
        for b in range(rows):
            valid = jnp.logical_and(row_of == b, position < filled)
            scores.append(jnp.where(valid, dot(query, kv_ref[0, b, :, cols], NT) * HD**-0.5, NEG))
        top = functools.reduce(jnp.maximum, [jnp.max(x, axis=1, keepdims=True) for x in scores])
        total = jnp.zeros((count, 1), jnp.float32)
        mixed = jnp.zeros((count, HD), jnp.float32)
        for b in range(rows):
            weight = jnp.exp(scores[b] - top)
            total = total + jnp.sum(weight, axis=1, keepdims=True)
            high = weight.astype(jnp.bfloat16)
            low = (weight - high.astype(jnp.float32)).astype(jnp.bfloat16)
            values = kv_ref[1, b, :, cols]
            mixed = mixed + dot(high, values) + dot(low, values)
        acc_out[g] = mixed
        top_out[g] = jnp.broadcast_to(top, (count, HD))
        sum_out[g] = jnp.broadcast_to(total, (count, HD))
    for copy in copies[3:]:
        copy.wait()


def early_kernel(blocks, chunk, place_ref, base_hbm, *refs):
    x_refs, refs = refs[:blocks], refs[blocks:]
    if blocks == 2:
        x_refs, refs = x_refs + refs[:1], refs[1:]
    a_refs, (out_ref, x_out, base_ref, sems) = refs[:-4], refs[-4:]
    columns, slab, ranks = base_hbm.shape[2], a_refs[0].shape[2], a_refs[0].shape[1]
    rows, steps, wide = x_refs[0].shape
    first = pl.multiple_of(place_ref[len(a_refs) + 1] * wide, wide)
    copies = []
    for i in range(wide // chunk):
        for m in range(2):
            copies.append(
                pltpu.make_async_copy(
                    base_hbm.at[m, pl.ds(first + i * chunk, chunk)],
                    base_ref.at[m, pl.ds(i * chunk, chunk)],
                    sems.at[2 * i + m],
                )
            )
    for copy in copies:
        copy.start()
    moved = place_ref[len(a_refs)] == 1
    for k in range(blocks):
        pieces = []
        for b in range(rows):
            x = x_refs[k][b].astype(jnp.float32)
            if len(x_refs) > blocks:
                x = jnp.where(moved, x_refs[k + 1][b].astype(jnp.float32), x)
            pieces.append(x)
        x = jnp.concatenate(pieces, axis=0)
        x_out[k * rows * steps : (k + 1) * rows * steps] = x.astype(jnp.bfloat16)
    count = blocks * rows * steps
    for m in range(2):
        total = jnp.zeros((count, ranks), jnp.float32)
        for i, a in enumerate(a_refs):
            start = pl.multiple_of(place_ref[i] * slab, slab)
            total = total + dot(x_out[:, pl.ds(start, slab)], a[m], NT)
        out_ref[:, 2 * columns + m * ranks : 2 * columns + (m + 1) * ranks] = total
    totals = [jnp.zeros((count, columns), jnp.float32) for _ in range(2)]
    for i in range(wide // chunk):
        at = slice(i * chunk, (i + 1) * chunk)
        for m in range(2):
            copies[2 * i + m].wait()
            totals[m] = totals[m] + dot(x_out[:, at], base_ref[m, at])
    for m in range(2):
        out_ref[:, m * columns : (m + 1) * columns] = totals[m]


def late_kernel(blocks, columns, place_ref, part_ref, x_ref, *refs):
    a_refs, outs = refs[:-blocks], refs[-blocks:]
    tokens = outs[0].shape[0]
    slab, ranks = a_refs[0].shape[2], a_refs[0].shape[1]
    sums = [part_ref[:, : 2 * columns]]
    for m in range(2):
        total = part_ref[:, 2 * columns + m * ranks : 2 * columns + (m + 1) * ranks]
        for i, a in enumerate(a_refs):
            start = pl.multiple_of(place_ref[i] * slab, slab)
            total = total + dot(x_ref[:, pl.ds(start, slab)], a[m], NT)
        sums.append(total)
    whole = jnp.concatenate(sums, axis=1)
    for j, out in enumerate(outs):
        out[...] = whole[j * tokens : (j + 1) * tokens].astype(out.dtype)


def collect_kernel(*refs):
    rows = refs[0].shape[1]
    for k, ref in enumerate(refs[:-1]):
        refs[-1][:, k * rows : (k + 1) * rows] = ref[...]


def order_kernel(count, place_ref, *refs):
    out = refs[-1]
    rows = refs[0].shape[1] // count
    for i, ref in enumerate(refs[:-1]):
        for k in range(count):
            start = pl.multiple_of(place_ref[i * count + k] * rows, rows)
            out[:, pl.ds(start, rows)] = ref[:, k * rows : (k + 1) * rows]


def rank_kernel(columns, mine_ref, *refs):
    total = mine_ref[:, 2 * columns :]
    for other in refs[:-1]:
        total = total + other[:, 2 * columns :].astype(jnp.float32)
    refs[-1][...] = total.astype(jnp.bfloat16)


def final_kernel(blocks, steps, group, place_ref, mine_ref, *refs):
    others, refs = refs[: blocks - 1], refs[blocks - 1 :]
    rank_refs, refs = refs[:blocks], refs[blocks:]
    up_ref, q_ref, acc_ref, top_ref, sum_ref, fresh_out, out = refs
    tokens, columns = mine_ref.shape[0], fresh_out.shape[3]
    rows, heads = tokens // steps, columns // HD
    ranks = rank_refs[0].shape[1] // 2
    fresh = []
    for m in range(2):
        cols = slice(m * columns, (m + 1) * columns)
        total = mine_ref[:, cols]
        for other in others:
            total = total + other[:, cols].astype(jnp.float32)
        for i, rank in enumerate(rank_refs):
            start = pl.multiple_of(place_ref[i] * ranks, ranks)
            total = total + dot(rank[:, m * ranks : (m + 1) * ranks], up_ref[m, pl.ds(start, ranks)])
        for b in range(rows):
            fresh_out[m, b] = total[b * steps : (b + 1) * steps].astype(jnp.bfloat16)
        fresh.append(total.astype(jnp.bfloat16))
    count = group * tokens
    token = lax.broadcasted_iota(jnp.int32, (count, tokens), 0) % tokens
    key = lax.broadcasted_iota(jnp.int32, (count, tokens), 1)
    valid = jnp.logical_and(token // steps == key // steps, key <= token)
    for g in range(heads):
        cols = slice(g * HD, (g + 1) * HD)
        scores = jnp.where(valid, dot(q_ref[g], fresh[0][:, cols], NT) * HD**-0.5, NEG)
        top_old = top_ref[g][:, :1]
        top = jnp.maximum(top_old, jnp.max(scores, axis=1, keepdims=True))
        scale = jnp.exp(top_old - top)
        weight = jnp.where(valid, jnp.exp(scores - top), 0.0)
        total = sum_ref[g][:, :1] * scale + jnp.sum(weight, axis=1, keepdims=True)
        weight = (weight / total).astype(jnp.bfloat16)
        mixed = acc_ref[g] * (scale / total) + dot(weight, fresh[1][:, cols])
        for h in range(group):
            lanes = slice((g * group + h) * HD, (g * group + h + 1) * HD)
            for b in range(rows):
                at = h * tokens + b * steps
                out[b, :, lanes] = mixed[at : at + steps].astype(jnp.bfloat16)


def smem():
    return pl.BlockSpec(memory_space=pltpu.SMEM)


def local(sizes, inputs, queries, kv_cache, lengths, base, a_factor, b_factor):
    fsdp, tp, sub = sizes
    inner = fsdp // tp
    row_count, steps, wide = inputs.shape
    tokens, columns, ranks = row_count * steps, base.shape[2], a_factor.shape[1]
    heads, group = columns // HD, QH // KVH
    f, t, s = lax.axis_index("fsdp"), lax.axis_index("tp"), lax.axis_index("sub")
    p, r = f // inner, f % inner
    bf16, f32 = jnp.bfloat16, jnp.float32

    def over_fsdp(x, k):
        return lax.ppermute(x, "fsdp", [(i, i ^ k) for i in range(fsdp)])

    def over_sub(x, k):
        return lax.ppermute(x, "sub", [(i, i ^ k) for i in range(sub)])

    def spread(x, k):
        pairs = []
        for i in range(fsdp):
            for j in range(tp):
                pairs.append((i * tp + j, (j * inner + i % inner) * tp + (i // inner + k) % tp))
        return lax.ppermute(x, ("fsdp", "tp"), pairs)

    if tp == 2:
        pairs = [(i * tp + i // inner, i * tp + 1 - i // inner) for i in range(fsdp)]
        near_x = spread(inputs, 1)
        xs = [inputs, near_x, lax.ppermute(near_x, ("fsdp", "tp"), pairs)]
    else:
        xs = jnp.stack([spread(inputs, k) for k in range(tp)])
        xs = [lax.dynamic_index_in_dim(xs, (t - p - j) % tp, keepdims=False) for j in range(tp)]

    far = [over_fsdp(a_factor, k) for k in range(1, inner)]
    near = [(0, e, over_sub(a_factor, e)) for e in range(1, sub)]

    def join(mine, other, bit):
        low = jnp.where(bit == 0, mine, other)
        high = jnp.where(bit == 0, other, mine)
        return jnp.concatenate([low, high], axis=1)

    def gather(x, axis, index, start, stop):
        size = {"fsdp": fsdp, "sub": sub}[axis]
        while start < stop:
            other = lax.ppermute(x, axis, [(i, i ^ start) for i in range(size)])
            x = join(x, other, (index // start) % 2)
            start = start * 2
        return x

    up = b_factor.transpose(0, 2, 1)
    direct = fsdp <= 4 and up.shape[1] % 16 == 0
    if direct:
        up = [up] + [over_fsdp(up, k) for k in range(1, fsdp)]
    else:
        up = gather(gather(up[:, None], "fsdp", f, 1, fsdp), "sub", s, 1, sub)
        up = up.reshape(2, sub, fsdp, -1, columns).swapaxes(1, 2).reshape(2, -1, columns)

    count = group * tokens
    per_head = jax.ShapeDtypeStruct((heads, count, HD), f32)
    *state, near_a = pl.pallas_call(
        functools.partial(cache_kernel, group),
        out_shape=[
            jax.ShapeDtypeStruct((heads, count, HD), bf16),
            per_head,
            per_head,
            per_head,
            jax.ShapeDtypeStruct(a_factor.shape, bf16),
        ],
        in_specs=[smem()] + [pl.BlockSpec(memory_space=pltpu.HBM)] * 3,
        out_specs=[vmem()] * 5,
        scratch_shapes=[
            pltpu.VMEM(queries.shape, bf16),
            pltpu.VMEM(kv_cache.shape, bf16),
            pltpu.SemaphoreType.DMA((4,)),
        ],
        compiler_params=params(40),
        cost_estimate=cost(C_CACHED),
        name="cached",
    )(lengths, queries, kv_cache, a_factor)

    def place_of(items):
        return [((r ^ k) * sub + (s ^ e)).astype(jnp.int32) for k, e, _ in items]

    xs, near_a = lax.optimization_barrier((xs, near_a))
    near = [(0, 0, near_a)] + near
    width = 2 * columns + 2 * ranks
    part, x = pl.pallas_call(
        functools.partial(early_kernel, tp, wide // 4),
        out_shape=[
            jax.ShapeDtypeStruct((tp * tokens, width), f32),
            jax.ShapeDtypeStruct((tp * tokens, wide), bf16),
        ],
        in_specs=[smem(), pl.BlockSpec(memory_space=pltpu.HBM)] + [vmem()] * (len(xs) + len(near)),
        out_specs=[vmem()] * 2,
        scratch_shapes=[pltpu.VMEM((2, wide, columns), bf16), pltpu.SemaphoreType.DMA((8,))],
        compiler_params=params(50),
        cost_estimate=cost(C_EARLY),
        name="early",
    )(jnp.stack(place_of(near) + [(t != p).astype(jnp.int32), p.astype(jnp.int32)]), base, *xs, *[a for _, _, a in near])

    far, part, up = lax.optimization_barrier((far, part, up))
    late_at = [(k, e) for k in range(1, inner) for e in range(sub)]
    late = [over_sub(far[k - 1], e) if e else far[k - 1] for k, e in late_at]
    parts = pl.pallas_call(
        functools.partial(late_kernel, tp, columns),
        out_shape=[jax.ShapeDtypeStruct((tokens, width), f32 if j == 0 else bf16) for j in range(tp)],
        in_specs=[smem()] + [vmem()] * (2 + len(late)),
        out_specs=[vmem()] * tp,
        compiler_params=params(),
        name="late",
    )(jnp.stack(place_of([(k, e, None) for k, e in late_at])), part, x, *late)

    parts, up = lax.optimization_barrier((parts, up))
    others = []
    for j in range(1, tp):
        pairs = [(i, (i + j * inner) % fsdp) for i in range(fsdp)]
        others.append(lax.ppermute(parts[j], "fsdp", pairs))

    if direct:
        piece = up[0].shape
        mine = pl.pallas_call(
            collect_kernel,
            out_shape=jax.ShapeDtypeStruct((2, fsdp * piece[1], columns), bf16),
            in_specs=[vmem()] * fsdp,
            out_specs=vmem(),
            compiler_params=params(),
            name="collect",
        )(*up)
        up = [mine] + [over_sub(mine, e) for e in range(1, sub)]
        place = [(f ^ k) * sub + (s ^ e) for e in range(sub) for k in range(fsdp)]
        up = pl.pallas_call(
            functools.partial(order_kernel, fsdp),
            out_shape=jax.ShapeDtypeStruct((2, sub * fsdp * piece[1], columns), bf16),
            in_specs=[smem()] + [vmem()] * sub,
            out_specs=vmem(),
            compiler_params=params(),
            name="order",
        )(jnp.stack(place).astype(jnp.int32), *up)

    own = pl.pallas_call(
        functools.partial(rank_kernel, columns),
        out_shape=jax.ShapeDtypeStruct((tokens, 2 * ranks), bf16),
        in_specs=[vmem()] * tp,
        out_specs=vmem(),
        compiler_params=params(),
        name="ranks",
    )(parts[0], *others)
    rank_parts = [own]
    for i in range(1, tp):
        rank_parts.append(lax.ppermute(own, "tp", [(j, (j + i) % tp) for j in range(tp)]))
    rank_place = jnp.stack([((t - i + tp) % tp).astype(jnp.int32) for i in range(tp)])

    fresh, attended = pl.pallas_call(
        functools.partial(final_kernel, tp, steps, group),
        out_shape=(
            jax.ShapeDtypeStruct((2, row_count, steps, columns), bf16),
            jax.ShapeDtypeStruct(queries.shape, bf16),
        ),
        in_specs=[smem()] + [vmem()] * (2 * tp + 5),
        out_specs=[vmem(), vmem()],
        compiler_params=params(),
        name="final",
    )(rank_place, parts[0], *others, *rank_parts, up, *state)
    return fresh, attended


def solution(mesh):
    sizes = tuple(mesh.shape[axis] for axis in ("fsdp", "tp", "sub"))
    return jax.shard_map(
        functools.partial(local, sizes),
        mesh=mesh,
        in_specs=(
            P(("groups", "fsdp", "sub"), None, "tp"),
            P(("groups", "fsdp", "sub"), None, "tp"),
            P(None, ("groups", "fsdp", "sub"), None, "tp"),
            P(("groups", "fsdp", "sub")),
            P(None, None, "tp"),
            P(None, "tp", ("fsdp", "sub")),
            P(None, "tp", ("fsdp", "sub")),
        ),
        out_specs=(
            P(None, ("groups", "fsdp", "sub"), None, "tp"),
            P(("groups", "fsdp", "sub"), None, "tp"),
        ),
        check_vma=False,
    )
```

```python
import functools

import jax
import jax.numpy as jnp
from jax import lax
from jax.experimental import pallas as pl
from jax.experimental.pallas import tpu as pltpu
from jax.sharding import PartitionSpec as P

HD = 128
KVH = 4
QH = 32

C_CACHED = 2.0
C_EARLY = 3.0
NEG = -1e30

NT = (((1,), (1,)), ((), ()))
NN = (((1,), (0,)), ((), ()))


def dot(x, y, dims=NN):
    return lax.dot_general(x, y, dims, preferred_element_type=jnp.float32)


def cost(us):
    return pl.CostEstimate(flops=int(us * 1e9), bytes_accessed=int(us * 3e6), transcendentals=0)


def vmem():
    return pl.BlockSpec(memory_space=pltpu.VMEM)


def params(mib=40):
    return pltpu.CompilerParams(vmem_limit_bytes=mib * 2**20)


def cache_kernel(
    group, count_up, len_ref, tick_ref, q_hbm, kv_hbm, *refs
):
    up_refs, refs = refs[:count_up], refs[count_up:]
    q_out, acc_out, top_out, sum_out, up_out, q_ref, kv_ref, sems = refs
    held = up_refs[0].shape[1]
    for i, up_ref in enumerate(up_refs):
        up_out[:, i * held : (i + 1) * held] = up_ref[...]
    copies = [
        pltpu.make_async_copy(q_hbm, q_ref, sems.at[0]),
        pltpu.make_async_copy(kv_hbm.at[0], kv_ref.at[0], sems.at[1]),
        pltpu.make_async_copy(kv_hbm.at[1], kv_ref.at[1], sems.at[2]),
    ]
    for copy in copies:
        copy.start()
    for copy in copies:
        copy.wait()
    rows, steps, width = q_ref.shape
    heads, cached = width // (group * HD), kv_ref.shape[2]
    tokens = rows * steps
    flat = jnp.concatenate([q_ref[b].astype(jnp.float32) for b in range(rows)], axis=0)
    flat = flat.astype(jnp.bfloat16)
    count = group * tokens
    row_of = (lax.broadcasted_iota(jnp.int32, (count, 1), 0) % tokens) // steps
    filled = jnp.zeros((count, 1), jnp.int32)
    for b in range(rows):
        filled = jnp.where(row_of == b, len_ref[b], filled)
    position = lax.broadcasted_iota(jnp.int32, (count, cached), 1)
    for g in range(heads):
        query = jnp.concatenate(
            [flat[:, (g * group + h) * HD : (g * group + h + 1) * HD] for h in range(group)], axis=0
        )
        q_out[g] = query
        cols = slice(g * HD, (g + 1) * HD)
        scores = []
        for b in range(rows):
            valid = jnp.logical_and(row_of == b, position < filled)
            scores.append(jnp.where(valid, dot(query, kv_ref[0, b, :, cols], NT) * HD**-0.5, NEG))
        top = functools.reduce(jnp.maximum, [jnp.max(x, axis=1, keepdims=True) for x in scores])
        total = jnp.zeros((count, 1), jnp.float32)
        mixed = jnp.zeros((count, HD), jnp.float32)
        for b in range(rows):
            weight = jnp.exp(scores[b] - top)
            total = total + jnp.sum(weight, axis=1, keepdims=True)
            high = weight.astype(jnp.bfloat16)
            low = (weight - high.astype(jnp.float32)).astype(jnp.bfloat16)
            values = kv_ref[1, b, :, cols]
            mixed = mixed + dot(high, values) + dot(low, values)
        acc_out[g] = mixed
        top_out[g] = jnp.broadcast_to(top, (count, HD))
        sum_out[g] = jnp.broadcast_to(total, (count, HD))


def early_kernel(blocks, chunk, place_ref, base_hbm, *refs):
    x_refs, refs = refs[:blocks], refs[blocks:]
    if blocks == 2:
        x_refs, refs = x_refs + refs[:1], refs[1:]
    a_refs, (out_ref, x_out, base_ref, sems) = refs[:-4], refs[-4:]
    columns, slab, ranks = base_hbm.shape[2], a_refs[0].shape[2], a_refs[0].shape[1]
    rows, steps, wide = x_refs[0].shape
    first = pl.multiple_of(place_ref[len(a_refs) + 1] * wide, wide)
    copies = []
    for i in range(wide // chunk):
        for m in range(2):
            copies.append(
                pltpu.make_async_copy(
                    base_hbm.at[m, pl.ds(first + i * chunk, chunk)],
                    base_ref.at[m, pl.ds(i * chunk, chunk)],
                    sems.at[2 * i + m],
                )
            )
    for copy in copies:
        copy.start()
    moved = place_ref[len(a_refs)] == 1
    for k in range(blocks):
        pieces = []
        for b in range(rows):
            x = x_refs[k][b].astype(jnp.float32)
            if len(x_refs) > blocks:
                x = jnp.where(moved, x_refs[k + 1][b].astype(jnp.float32), x)
            pieces.append(x)
        x = jnp.concatenate(pieces, axis=0)
        x_out[k * rows * steps : (k + 1) * rows * steps] = x.astype(jnp.bfloat16)
    count = blocks * rows * steps
    for m in range(2):
        total = jnp.zeros((count, ranks), jnp.float32)
        for i, a in enumerate(a_refs):
            start = pl.multiple_of(place_ref[i] * slab, slab)
            total = total + dot(x_out[:, pl.ds(start, slab)], a[m], NT)
        out_ref[:, 2 * columns + m * ranks : 2 * columns + (m + 1) * ranks] = total
    totals = [jnp.zeros((count, columns), jnp.float32) for _ in range(2)]
    for i in range(wide // chunk):
        at = slice(i * chunk, (i + 1) * chunk)
        for m in range(2):
            copies[2 * i + m].wait()
            totals[m] = totals[m] + dot(x_out[:, at], base_ref[m, at])
    for m in range(2):
        out_ref[:, m * columns : (m + 1) * columns] = totals[m]


def late_kernel(blocks, columns, place_ref, part_ref, x_ref, *refs):
    a_refs, outs = refs[:-blocks], refs[-blocks:]
    tokens = outs[0].shape[0]
    slab, ranks = a_refs[0].shape[2], a_refs[0].shape[1]
    sums = [part_ref[:, : 2 * columns]]
    for m in range(2):
        total = part_ref[:, 2 * columns + m * ranks : 2 * columns + (m + 1) * ranks]
        for i, a in enumerate(a_refs):
            start = pl.multiple_of(place_ref[i] * slab, slab)
            total = total + dot(x_ref[:, pl.ds(start, slab)], a[m], NT)
        sums.append(total)
    whole = jnp.concatenate(sums, axis=1)
    for j, out in enumerate(outs):
        out[...] = whole[j * tokens : (j + 1) * tokens].astype(out.dtype)


def tick_kernel(out_ref):
    out_ref[...] = jnp.zeros(out_ref.shape, jnp.float32)


def collect_kernel(*refs):
    rows = refs[0].shape[1]
    for k, ref in enumerate(refs[:-1]):
        refs[-1][:, k * rows : (k + 1) * rows] = ref[...]


def order_kernel(count, place_ref, *refs):
    out = refs[-1]
    rows = refs[0].shape[1] // count
    for i, ref in enumerate(refs[:-1]):
        for k in range(count):
            start = pl.multiple_of(place_ref[i * count + k] * rows, rows)
            out[:, pl.ds(start, rows)] = ref[:, k * rows : (k + 1) * rows]


def rank_kernel(columns, mine_ref, *refs):
    total = mine_ref[:, 2 * columns :]
    for other in refs[:-1]:
        total = total + other[:, 2 * columns :].astype(jnp.float32)
    refs[-1][...] = total.astype(jnp.bfloat16)


def final_kernel(blocks, steps, group, place_ref, mine_ref, *refs):
    others, refs = refs[: blocks - 1], refs[blocks - 1 :]
    rank_refs, refs = refs[:blocks], refs[blocks:]
    up_ref, q_ref, acc_ref, top_ref, sum_ref, fresh_out, out = refs
    tokens, columns = mine_ref.shape[0], fresh_out.shape[3]
    rows, heads = tokens // steps, columns // HD
    ranks = rank_refs[0].shape[1] // 2
    fresh = []
    for m in range(2):
        cols = slice(m * columns, (m + 1) * columns)
        total = mine_ref[:, cols]
        for other in others:
            total = total + other[:, cols].astype(jnp.float32)
        for i, rank in enumerate(rank_refs):
            start = pl.multiple_of(place_ref[i] * ranks, ranks)
            total = total + dot(rank[:, m * ranks : (m + 1) * ranks], up_ref[m, pl.ds(start, ranks)])
        for b in range(rows):
            fresh_out[m, b] = total[b * steps : (b + 1) * steps].astype(jnp.bfloat16)
        fresh.append(total.astype(jnp.bfloat16))
    count = group * tokens
    token = lax.broadcasted_iota(jnp.int32, (count, tokens), 0) % tokens
    key = lax.broadcasted_iota(jnp.int32, (count, tokens), 1)
    valid = jnp.logical_and(token // steps == key // steps, key <= token)
    for g in range(heads):
        cols = slice(g * HD, (g + 1) * HD)
        scores = jnp.where(valid, dot(q_ref[g], fresh[0][:, cols], NT) * HD**-0.5, NEG)
        top_old = top_ref[g][:, :1]
        top = jnp.maximum(top_old, jnp.max(scores, axis=1, keepdims=True))
        scale = jnp.exp(top_old - top)
        weight = jnp.where(valid, jnp.exp(scores - top), 0.0)
        total = sum_ref[g][:, :1] * scale + jnp.sum(weight, axis=1, keepdims=True)
        weight = (weight / total).astype(jnp.bfloat16)
        mixed = acc_ref[g] * (scale / total) + dot(weight, fresh[1][:, cols])
        for h in range(group):
            lanes = slice((g * group + h) * HD, (g * group + h + 1) * HD)
            for b in range(rows):
                at = h * tokens + b * steps
                out[b, :, lanes] = mixed[at : at + steps].astype(jnp.bfloat16)


def smem():
    return pl.BlockSpec(memory_space=pltpu.SMEM)


def local(sizes, inputs, queries, kv_cache, lengths, base, a_factor, b_factor):
    fsdp, tp, sub = sizes
    inner = fsdp // tp
    row_count, steps, wide = inputs.shape
    tokens, columns, ranks = row_count * steps, base.shape[2], a_factor.shape[1]
    heads, group = columns // HD, QH // KVH
    f, t, s = lax.axis_index("fsdp"), lax.axis_index("tp"), lax.axis_index("sub")
    p, r = f // inner, f % inner
    bf16, f32 = jnp.bfloat16, jnp.float32

    def over_fsdp(x, k):
        return lax.ppermute(x, "fsdp", [(i, i ^ k) for i in range(fsdp)])

    def over_sub(x, k):
        return lax.ppermute(x, "sub", [(i, i ^ k) for i in range(sub)])

    def spread(x, k):
        pairs = []
        for i in range(fsdp):
            for j in range(tp):
                pairs.append((i * tp + j, (j * inner + i % inner) * tp + (i // inner + k) % tp))
        return lax.ppermute(x, ("fsdp", "tp"), pairs)

    xs = [spread(inputs, k) for k in range(1 if tp == 2 else 0, tp)]

    tick = pl.pallas_call(
        tick_kernel,
        out_shape=jax.ShapeDtypeStruct((8, 128), f32),
        out_specs=vmem(),
        cost_estimate=cost(8.0),
        name="tick",
    )()

    a_own, tick = lax.optimization_barrier((a_factor, tick))
    far = [over_fsdp(a_own, k) for k in range(1, inner)]
    near = [(0, e, over_sub(a_factor, e)) for e in range(1, sub)]

    def join(mine, other, bit):
        low = jnp.where(bit == 0, mine, other)
        high = jnp.where(bit == 0, other, mine)
        return jnp.concatenate([low, high], axis=1)

    def gather(x, axis, index, start, stop):
        size = {"fsdp": fsdp, "sub": sub}[axis]
        while start < stop:
            other = lax.ppermute(x, axis, [(i, i ^ start) for i in range(size)])
            x = join(x, other, (index // start) % 2)
            start = start * 2
        return x

    up = b_factor.transpose(0, 2, 1)
    direct = fsdp == 4 and inner == 2 and up.shape[1] % 16 == 0
    if direct:
        up = [up, over_fsdp(up, 1)]
    else:
        up = gather(gather(up[:, None], "fsdp", f, 1, fsdp), "sub", s, 1, sub)
        up = [up.reshape(2, sub, fsdp, -1, columns).swapaxes(1, 2).reshape(2, -1, columns)]

    count = group * tokens
    per_head = jax.ShapeDtypeStruct((heads, count, HD), f32)
    *state, up = pl.pallas_call(
        functools.partial(cache_kernel, group, len(up)),
        out_shape=[
            jax.ShapeDtypeStruct((heads, count, HD), bf16),
            per_head,
            per_head,
            per_head,
            jax.ShapeDtypeStruct((2, len(up) * up[0].shape[1], columns), bf16),
        ],
        in_specs=[smem(), vmem()] + [pl.BlockSpec(memory_space=pltpu.HBM)] * 2 + [vmem()] * len(up),
        out_specs=[vmem()] * 5,
        scratch_shapes=[
            pltpu.VMEM(queries.shape, bf16),
            pltpu.VMEM(kv_cache.shape, bf16),
            pltpu.SemaphoreType.DMA((3,)),
        ],
        compiler_params=params(40),
        cost_estimate=cost(C_CACHED),
        name="cached",
    )(lengths, tick, queries, kv_cache, *up)

    def place_of(items):
        return [((r ^ k) * sub + (s ^ e)).astype(jnp.int32) for k, e, _ in items]

    xs, near_a = lax.optimization_barrier((xs, up))
    if tp == 2:
        pairs = [(i * tp + i // inner, i * tp + 1 - i // inner) for i in range(fsdp)]
        xs = [inputs, xs[0], lax.ppermute(xs[0], ("fsdp", "tp"), pairs)]
    else:
        xs = jnp.stack(xs)
        xs = [lax.dynamic_index_in_dim(xs, (t - p - j) % tp, keepdims=False) for j in range(tp)]
    near = [(0, 0, a_factor)] + near
    up = [up, over_fsdp(up, inner)] if direct else [up]
    width = 2 * columns + 2 * ranks
    part, x = pl.pallas_call(
        functools.partial(early_kernel, tp, wide // 4),
        out_shape=[
            jax.ShapeDtypeStruct((tp * tokens, width), f32),
            jax.ShapeDtypeStruct((tp * tokens, wide), bf16),
        ],
        in_specs=[smem(), pl.BlockSpec(memory_space=pltpu.HBM)] + [vmem()] * (len(xs) + len(near)),
        out_specs=[vmem()] * 2,
        scratch_shapes=[pltpu.VMEM((2, wide, columns), bf16), pltpu.SemaphoreType.DMA((8,))],
        compiler_params=params(50),
        cost_estimate=cost(C_EARLY),
        name="early",
    )(jnp.stack(place_of(near) + [(t != p).astype(jnp.int32), p.astype(jnp.int32)]), base, *xs, *[a for _, _, a in near])

    far, part, up = lax.optimization_barrier((far, part, up))
    late_at = [(k, e) for k in range(1, inner) for e in range(sub)]
    late = [over_sub(far[k - 1], e) if e else far[k - 1] for k, e in late_at]
    parts = pl.pallas_call(
        functools.partial(late_kernel, tp, columns),
        out_shape=[jax.ShapeDtypeStruct((tokens, width), f32 if j == 0 else bf16) for j in range(tp)],
        in_specs=[smem()] + [vmem()] * (2 + len(late)),
        out_specs=[vmem()] * tp,
        compiler_params=params(),
        name="late",
    )(jnp.stack(place_of([(k, e, None) for k, e in late_at])), part, x, *late)

    parts, up = lax.optimization_barrier((parts, up))
    others = []
    for j in range(1, tp):
        pairs = [(i, (i + j * inner) % fsdp) for i in range(fsdp)]
        others.append(lax.ppermute(parts[j], "fsdp", pairs))

    if direct:
        rows_up = up[0].shape[1] * 2
        mine = pl.pallas_call(
            collect_kernel,
            out_shape=jax.ShapeDtypeStruct((2, rows_up, columns), bf16),
            in_specs=[vmem()] * 2,
            out_specs=vmem(),
            compiler_params=params(),
            name="collect",
        )(*up)
        up = [mine] + [over_sub(mine, e) for e in range(1, sub)]
        place = [(f ^ k) * sub + (s ^ e) for e in range(sub) for k in range(fsdp)]
        up = pl.pallas_call(
            functools.partial(order_kernel, fsdp),
            out_shape=jax.ShapeDtypeStruct((2, sub * rows_up, columns), bf16),
            in_specs=[smem()] + [vmem()] * sub,
            out_specs=vmem(),
            compiler_params=params(),
            name="order",
        )(jnp.stack(place).astype(jnp.int32), *up)
    else:
        up = up[0]

    own = pl.pallas_call(
        functools.partial(rank_kernel, columns),
        out_shape=jax.ShapeDtypeStruct((tokens, 2 * ranks), bf16),
        in_specs=[vmem()] * tp,
        out_specs=vmem(),
        compiler_params=params(),
        name="ranks",
    )(parts[0], *others)
    rank_parts = [own]
    for i in range(1, tp):
        rank_parts.append(lax.ppermute(own, "tp", [(j, (j + i) % tp) for j in range(tp)]))
    rank_place = jnp.stack([((t - i + tp) % tp).astype(jnp.int32) for i in range(tp)])

    fresh, attended = pl.pallas_call(
        functools.partial(final_kernel, tp, steps, group),
        out_shape=(
            jax.ShapeDtypeStruct((2, row_count, steps, columns), bf16),
            jax.ShapeDtypeStruct(queries.shape, bf16),
        ),
        in_specs=[smem()] + [vmem()] * (2 * tp + 5),
        out_specs=[vmem(), vmem()],
        compiler_params=params(),
        name="final",
    )(rank_place, parts[0], *others, *rank_parts, up, *state)
    return fresh, attended


def solution(mesh):
    sizes = tuple(mesh.shape[axis] for axis in ("fsdp", "tp", "sub"))
    return jax.shard_map(
        functools.partial(local, sizes),
        mesh=mesh,
        in_specs=(
            P(("groups", "fsdp", "sub"), None, "tp"),
            P(("groups", "fsdp", "sub"), None, "tp"),
            P(None, ("groups", "fsdp", "sub"), None, "tp"),
            P(("groups", "fsdp", "sub")),
            P(None, None, "tp"),
            P(None, "tp", ("fsdp", "sub")),
            P(None, "tp", ("fsdp", "sub")),
        ),
        out_specs=(
            P(None, ("groups", "fsdp", "sub"), None, "tp"),
            P(("groups", "fsdp", "sub"), None, "tp"),
        ),
        check_vma=False,
    )
```

```python
import functools

import jax
import jax.numpy as jnp
from jax import lax
from jax.experimental import pallas as pl
from jax.experimental.pallas import tpu as pltpu
from jax.sharding import PartitionSpec as P

HD = 128
KVH = 4
QH = 32

C_CACHED = 2.0
C_EARLY = 3.0
NEG = -1e30

NT = (((1,), (1,)), ((), ()))
NN = (((1,), (0,)), ((), ()))


def dot(x, y, dims=NN):
    return lax.dot_general(x, y, dims, preferred_element_type=jnp.float32)


def cost(us):
    return pl.CostEstimate(flops=int(us * 1e9), bytes_accessed=int(us * 3e6), transcendentals=0)


def places(sizes, items):
    row, core = lax.rem(lax.axis_index("fsdp"), sizes[0] // sizes[1]), lax.axis_index("sub")
    return [(row ^ k) * sizes[2] + (core ^ e) for k, e in items]


def vmem():
    return pl.BlockSpec(memory_space=pltpu.VMEM)


def params(mib=40):
    return pltpu.CompilerParams(vmem_limit_bytes=mib * 2**20)


def cache_kernel(
    group, count_up, len_ref, tick_ref, q_hbm, kv_hbm, *refs
):
    up_refs, refs = refs[:count_up], refs[count_up:]
    q_out, acc_out, top_out, sum_out, up_out, q_ref, kv_ref, sems = refs
    held = up_refs[0].shape[1]
    for i, up_ref in enumerate(up_refs):
        up_out[:, i * held : (i + 1) * held] = up_ref[...]
    copies = [
        pltpu.make_async_copy(q_hbm, q_ref, sems.at[0]),
        pltpu.make_async_copy(kv_hbm.at[0], kv_ref.at[0], sems.at[1]),
        pltpu.make_async_copy(kv_hbm.at[1], kv_ref.at[1], sems.at[2]),
    ]
    for copy in copies:
        copy.start()
    for copy in copies:
        copy.wait()
    rows, steps, width = q_ref.shape
    heads, cached = width // (group * HD), kv_ref.shape[2]
    tokens = rows * steps
    flat = jnp.concatenate([q_ref[b].astype(jnp.float32) for b in range(rows)], axis=0)
    flat = flat.astype(jnp.bfloat16)
    count = group * tokens
    row_of = (lax.broadcasted_iota(jnp.int32, (count, 1), 0) % tokens) // steps
    filled = jnp.zeros((count, 1), jnp.int32)
    for b in range(rows):
        filled = jnp.where(row_of == b, len_ref[b], filled)
    position = lax.broadcasted_iota(jnp.int32, (count, cached), 1)
    for g in range(heads):
        query = jnp.concatenate(
            [flat[:, (g * group + h) * HD : (g * group + h + 1) * HD] for h in range(group)], axis=0
        )
        q_out[g] = query
        cols = slice(g * HD, (g + 1) * HD)
        scores = []
        for b in range(rows):
            valid = jnp.logical_and(row_of == b, position < filled)
            scores.append(jnp.where(valid, dot(query, kv_ref[0, b, :, cols], NT) * HD**-0.5, NEG))
        top = functools.reduce(jnp.maximum, [jnp.max(x, axis=1, keepdims=True) for x in scores])
        total = jnp.zeros((count, 1), jnp.float32)
        mixed = jnp.zeros((count, HD), jnp.float32)
        for b in range(rows):
            weight = jnp.exp(scores[b] - top)
            total = total + jnp.sum(weight, axis=1, keepdims=True)
            high = weight.astype(jnp.bfloat16)
            low = (weight - high.astype(jnp.float32)).astype(jnp.bfloat16)
            values = kv_ref[1, b, :, cols]
            mixed = mixed + dot(high, values) + dot(low, values)
        acc_out[g] = mixed
        top_out[g] = jnp.broadcast_to(top, (count, HD))
        sum_out[g] = jnp.broadcast_to(total, (count, HD))


def early_kernel(blocks, chunk, sizes, items, base_hbm, *refs):
    x_refs, refs = refs[:blocks], refs[blocks:]
    if blocks == 2:
        x_refs, refs = x_refs + refs[:1], refs[1:]
    a_refs, (out_ref, x_out, base_ref, sems) = refs[:-4], refs[-4:]
    columns, slab, ranks = base_hbm.shape[2], a_refs[0].shape[2], a_refs[0].shape[1]
    rows, steps, wide = x_refs[0].shape
    block = lax.div(lax.axis_index("fsdp"), sizes[0] // sizes[1])
    place = places(sizes, items)
    first = pl.multiple_of(block * wide, wide)
    copies = []
    for i in range(wide // chunk):
        for m in range(2):
            copies.append(
                pltpu.make_async_copy(
                    base_hbm.at[m, pl.ds(first + i * chunk, chunk)],
                    base_ref.at[m, pl.ds(i * chunk, chunk)],
                    sems.at[2 * i + m],
                )
            )
    for copy in copies:
        copy.start()
    moved = lax.axis_index("tp") != block
    for k in range(blocks):
        pieces = []
        for b in range(rows):
            x = x_refs[k][b].astype(jnp.float32)
            if len(x_refs) > blocks:
                x = jnp.where(moved, x_refs[k + 1][b].astype(jnp.float32), x)
            pieces.append(x)
        x = jnp.concatenate(pieces, axis=0)
        x_out[k * rows * steps : (k + 1) * rows * steps] = x.astype(jnp.bfloat16)
    count = blocks * rows * steps
    total = jnp.zeros((count, 2 * ranks), jnp.float32)
    for i, a in enumerate(a_refs):
        start = pl.multiple_of(place[i] * slab, slab)
        total = total + dot(x_out[:, pl.ds(start, slab)], a[...].reshape(2 * ranks, slab), NT)
    out_ref[:, 2 * columns :] = total
    totals = [jnp.zeros((count, columns), jnp.float32) for _ in range(2)]
    for i in range(wide // chunk):
        at = slice(i * chunk, (i + 1) * chunk)
        for m in range(2):
            copies[2 * i + m].wait()
            totals[m] = totals[m] + dot(x_out[:, at], base_ref[m, at])
    for m in range(2):
        out_ref[:, m * columns : (m + 1) * columns] = totals[m]


def late_kernel(blocks, columns, sizes, items, part_ref, x_ref, *refs):
    a_refs, outs = refs[:-blocks], refs[-blocks:]
    tokens = outs[0].shape[0]
    slab, ranks = a_refs[0].shape[2], a_refs[0].shape[1]
    place = places(sizes, items)
    total = part_ref[:, 2 * columns :]
    for i, a in enumerate(a_refs):
        start = pl.multiple_of(place[i] * slab, slab)
        total = total + dot(x_ref[:, pl.ds(start, slab)], a[...].reshape(2 * ranks, slab), NT)
    for j, out in enumerate(outs):
        at = slice(j * tokens, (j + 1) * tokens)
        out[:, : 2 * columns] = part_ref[at, : 2 * columns].astype(out.dtype)
        out[:, 2 * columns :] = total[at].astype(out.dtype)


def tick_kernel(out_ref):
    out_ref[...] = jnp.zeros(out_ref.shape, jnp.float32)


def collect_kernel(*refs):
    rows = refs[0].shape[1]
    for k, ref in enumerate(refs[:-1]):
        refs[-1][:, k * rows : (k + 1) * rows] = ref[...]


def order_kernel(count, cores, *refs):
    out = refs[-1]
    f, s = lax.axis_index("fsdp"), lax.axis_index("sub")
    rows = refs[0].shape[1] // count
    for i, ref in enumerate(refs[:-1]):
        for k in range(count):
            start = pl.multiple_of(((f ^ k) * cores + (s ^ i)) * rows, rows)
            out[:, pl.ds(start, rows)] = ref[:, k * rows : (k + 1) * rows]


def rank_kernel(columns, mine_ref, *refs):
    total = mine_ref[:, 2 * columns :]
    for other in refs[:-1]:
        total = total + other[:, 2 * columns :].astype(jnp.float32)
    refs[-1][...] = total.astype(jnp.bfloat16)


def first_kernel(blocks, mine_ref, *refs):
    others, (rank_ref, up_ref, out_ref) = refs[: blocks - 1], refs[blocks - 1 :]
    columns, ranks = up_ref.shape[2], rank_ref.shape[1] // 2
    start = pl.multiple_of(lax.axis_index("tp") * ranks, ranks)
    for m in range(2):
        cols = slice(m * columns, (m + 1) * columns)
        total = mine_ref[:, cols]
        for other in others:
            total = total + other[:, cols].astype(jnp.float32)
        rank = rank_ref[:, m * ranks : (m + 1) * ranks]
        out_ref[:, cols] = total + dot(rank, up_ref[m, pl.ds(start, ranks)])


def final_kernel(blocks, steps, group, sum_in, *refs):
    rank_refs, refs = refs[: blocks - 1], refs[blocks - 1 :]
    up_ref, q_ref, acc_ref, top_ref, sum_ref, fresh_out, out = refs
    tokens, columns = sum_in.shape[0], fresh_out.shape[3]
    rows, heads = tokens // steps, columns // HD
    ranks = rank_refs[0].shape[1] // 2
    fresh = []
    for m in range(2):
        total = sum_in[:, m * columns : (m + 1) * columns]
        for i, rank in enumerate(rank_refs):
            other = lax.rem(lax.axis_index("tp") - (i + 1) + blocks, blocks)
            start = pl.multiple_of(other * ranks, ranks)
            total = total + dot(rank[:, m * ranks : (m + 1) * ranks], up_ref[m, pl.ds(start, ranks)])
        for b in range(rows):
            fresh_out[m, b] = total[b * steps : (b + 1) * steps].astype(jnp.bfloat16)
        fresh.append(total.astype(jnp.bfloat16))
    count = group * tokens
    token = lax.broadcasted_iota(jnp.int32, (count, tokens), 0) % tokens
    key = lax.broadcasted_iota(jnp.int32, (count, tokens), 1)
    valid = jnp.logical_and(token // steps == key // steps, key <= token)
    for g in range(heads):
        cols = slice(g * HD, (g + 1) * HD)
        scores = jnp.where(valid, dot(q_ref[g], fresh[0][:, cols], NT) * HD**-0.5, NEG)
        top_old = top_ref[g][:, :1]
        top = jnp.maximum(top_old, jnp.max(scores, axis=1, keepdims=True))
        scale = jnp.exp(top_old - top)
        weight = jnp.where(valid, jnp.exp(scores - top), 0.0)
        total = sum_ref[g][:, :1] * scale + jnp.sum(weight, axis=1, keepdims=True)
        weight = (weight / total).astype(jnp.bfloat16)
        mixed = acc_ref[g] * (scale / total) + dot(weight, fresh[1][:, cols])
        for h in range(group):
            lanes = slice((g * group + h) * HD, (g * group + h + 1) * HD)
            for b in range(rows):
                at = h * tokens + b * steps
                out[b, :, lanes] = mixed[at : at + steps].astype(jnp.bfloat16)


def smem():
    return pl.BlockSpec(memory_space=pltpu.SMEM)


def local(sizes, inputs, queries, kv_cache, lengths, base, a_factor, b_factor):
    fsdp, tp, sub = sizes
    inner = fsdp // tp
    row_count, steps, wide = inputs.shape
    tokens, columns, ranks = row_count * steps, base.shape[2], a_factor.shape[1]
    heads, group = columns // HD, QH // KVH
    f, t, s = lax.axis_index("fsdp"), lax.axis_index("tp"), lax.axis_index("sub")
    p, r = f // inner, f % inner
    bf16, f32 = jnp.bfloat16, jnp.float32

    def over_fsdp(x, k):
        return lax.ppermute(x, "fsdp", [(i, i ^ k) for i in range(fsdp)])

    def over_sub(x, k):
        return lax.ppermute(x, "sub", [(i, i ^ k) for i in range(sub)])

    def spread(x, k):
        pairs = []
        for i in range(fsdp):
            for j in range(tp):
                pairs.append((i * tp + j, (j * inner + i % inner) * tp + (i // inner + k) % tp))
        return lax.ppermute(x, ("fsdp", "tp"), pairs)

    xs = [spread(inputs, k) for k in range(1 if tp == 2 else 0, tp)]

    tick = pl.pallas_call(
        tick_kernel,
        out_shape=jax.ShapeDtypeStruct((8, 128), f32),
        out_specs=vmem(),
        cost_estimate=cost(8.0),
        name="tick",
    )()

    a_own, tick = lax.optimization_barrier((a_factor, tick))
    far = [over_fsdp(a_own, k) for k in range(1, inner)]
    near = [(0, e, over_sub(a_factor, e)) for e in range(1, sub)]

    def join(mine, other, bit):
        low = jnp.where(bit == 0, mine, other)
        high = jnp.where(bit == 0, other, mine)
        return jnp.concatenate([low, high], axis=1)

    def gather(x, axis, index, start, stop):
        size = {"fsdp": fsdp, "sub": sub}[axis]
        while start < stop:
            other = lax.ppermute(x, axis, [(i, i ^ start) for i in range(size)])
            x = join(x, other, (index // start) % 2)
            start = start * 2
        return x

    up = b_factor.transpose(0, 2, 1)
    direct = fsdp == 4 and inner == 2 and up.shape[1] % 16 == 0
    if direct:
        up = [up, over_fsdp(up, 1)]
    else:
        up = gather(gather(up[:, None], "fsdp", f, 1, fsdp), "sub", s, 1, sub)
        up = [up.reshape(2, sub, fsdp, -1, columns).swapaxes(1, 2).reshape(2, -1, columns)]

    count = group * tokens
    per_head = jax.ShapeDtypeStruct((heads, count, HD), f32)
    *state, up = pl.pallas_call(
        functools.partial(cache_kernel, group, len(up)),
        out_shape=[
            jax.ShapeDtypeStruct((heads, count, HD), bf16),
            per_head,
            per_head,
            per_head,
            jax.ShapeDtypeStruct((2, len(up) * up[0].shape[1], columns), bf16),
        ],
        in_specs=[smem(), vmem()] + [pl.BlockSpec(memory_space=pltpu.HBM)] * 2 + [vmem()] * len(up),
        out_specs=[vmem()] * 5,
        scratch_shapes=[
            pltpu.VMEM(queries.shape, bf16),
            pltpu.VMEM(kv_cache.shape, bf16),
            pltpu.SemaphoreType.DMA((3,)),
        ],
        compiler_params=params(40),
        cost_estimate=cost(C_CACHED),
        name="cached",
    )(lengths, tick, queries, kv_cache, *up)

    xs, near_a = lax.optimization_barrier((xs, up))
    if tp == 2:
        pairs = [(i * tp + i // inner, i * tp + 1 - i // inner) for i in range(fsdp)]
        xs = [inputs, xs[0], lax.ppermute(xs[0], ("fsdp", "tp"), pairs)]
    else:
        xs = jnp.stack(xs)
        xs = [lax.dynamic_index_in_dim(xs, (t - p - j) % tp, keepdims=False) for j in range(tp)]
    near = [(0, 0, a_factor)] + near
    up = [up, over_fsdp(up, inner)] if direct else [up]
    width = 2 * columns + 2 * ranks
    part, x = pl.pallas_call(
        functools.partial(early_kernel, tp, wide // 4, sizes, [(k, e) for k, e, _ in near]),
        out_shape=[
            jax.ShapeDtypeStruct((tp * tokens, width), f32),
            jax.ShapeDtypeStruct((tp * tokens, wide), bf16),
        ],
        in_specs=[pl.BlockSpec(memory_space=pltpu.HBM)] + [vmem()] * (len(xs) + len(near)),
        out_specs=[vmem()] * 2,
        scratch_shapes=[pltpu.VMEM((2, wide, columns), bf16), pltpu.SemaphoreType.DMA((8,))],
        compiler_params=params(50),
        cost_estimate=cost(C_EARLY),
        name="early",
    )(base, *xs, *[a for _, _, a in near])

    far, part, up = lax.optimization_barrier((far, part, up))
    late_at = [(k, e) for k in range(1, inner) for e in range(sub)]
    late = [over_sub(far[k - 1], e) if e else far[k - 1] for k, e in late_at]
    parts = pl.pallas_call(
        functools.partial(late_kernel, tp, columns, sizes, late_at),
        out_shape=[jax.ShapeDtypeStruct((tokens, width), f32 if j == 0 else bf16) for j in range(tp)],
        in_specs=[vmem()] * (2 + len(late)),
        out_specs=[vmem()] * tp,
        compiler_params=params(),
        name="late",
    )(part, x, *late)

    parts, up = lax.optimization_barrier((parts, up))
    others = []
    for j in range(1, tp):
        pairs = [(i, (i + j * inner) % fsdp) for i in range(fsdp)]
        others.append(lax.ppermute(parts[j], "fsdp", pairs))

    if direct:
        rows_up = up[0].shape[1] * 2
        mine = pl.pallas_call(
            collect_kernel,
            out_shape=jax.ShapeDtypeStruct((2, rows_up, columns), bf16),
            in_specs=[vmem()] * 2,
            out_specs=vmem(),
            compiler_params=params(),
            name="collect",
        )(*up)
        up = [mine] + [over_sub(mine, e) for e in range(1, sub)]
        up = pl.pallas_call(
            functools.partial(order_kernel, fsdp, sub),
            out_shape=jax.ShapeDtypeStruct((2, sub * rows_up, columns), bf16),
            in_specs=[vmem()] * sub,
            out_specs=vmem(),
            compiler_params=params(),
            name="order",
        )(*up)
    else:
        up = up[0]

    own = pl.pallas_call(
        functools.partial(rank_kernel, columns),
        out_shape=jax.ShapeDtypeStruct((tokens, 2 * ranks), bf16),
        in_specs=[vmem()] * tp,
        out_specs=vmem(),
        compiler_params=params(),
        name="ranks",
    )(parts[0], *others)
    rank_parts = [own]
    for i in range(1, tp):
        rank_parts.append(lax.ppermute(own, "tp", [(j, (j + i) % tp) for j in range(tp)]))

    first = pl.pallas_call(
        functools.partial(first_kernel, tp),
        out_shape=jax.ShapeDtypeStruct((tokens, 2 * columns), f32),
        in_specs=[vmem()] * (tp + 2),
        out_specs=vmem(),
        compiler_params=params(),
        name="first",
    )(parts[0], *others, own, up)
    fresh, attended = pl.pallas_call(
        functools.partial(final_kernel, tp, steps, group),
        out_shape=(
            jax.ShapeDtypeStruct((2, row_count, steps, columns), bf16),
            jax.ShapeDtypeStruct(queries.shape, bf16),
        ),
        in_specs=[vmem()] * (tp + 5),
        out_specs=[vmem(), vmem()],
        compiler_params=params(),
        name="final",
    )(first, *rank_parts[1:], up, *state)
    return fresh, attended


def solution(mesh):
    sizes = tuple(mesh.shape[axis] for axis in ("fsdp", "tp", "sub"))
    return jax.shard_map(
        functools.partial(local, sizes),
        mesh=mesh,
        in_specs=(
            P(("groups", "fsdp", "sub"), None, "tp"),
            P(("groups", "fsdp", "sub"), None, "tp"),
            P(None, ("groups", "fsdp", "sub"), None, "tp"),
            P(("groups", "fsdp", "sub")),
            P(None, None, "tp"),
            P(None, "tp", ("fsdp", "sub")),
            P(None, "tp", ("fsdp", "sub")),
        ),
        out_specs=(
            P(None, ("groups", "fsdp", "sub"), None, "tp"),
            P(("groups", "fsdp", "sub"), None, "tp"),
        ),
        check_vma=False,
    )
```

```python
import functools

import jax
import jax.numpy as jnp
from jax import lax
from jax.experimental import pallas as pl
from jax.experimental.pallas import tpu as pltpu
from jax.sharding import PartitionSpec as P

HD = 128
KVH = 4
QH = 32

C_CACHED = 2.0
C_EARLY = 3.0
NEG = -1e30

NT = (((1,), (1,)), ((), ()))
NN = (((1,), (0,)), ((), ()))


def dot(x, y, dims=NN):
    return lax.dot_general(x, y, dims, preferred_element_type=jnp.float32)


def cost(us):
    return pl.CostEstimate(flops=int(us * 1e9), bytes_accessed=int(us * 3e6), transcendentals=0)


def places(sizes, items):
    row, core = lax.rem(lax.axis_index("fsdp"), sizes[0] // sizes[1]), lax.axis_index("sub")
    return [(row ^ k) * sizes[2] + (core ^ e) for k, e in items]


def vmem():
    return pl.BlockSpec(memory_space=pltpu.VMEM)


def params(mib=40):
    return pltpu.CompilerParams(vmem_limit_bytes=mib * 2**20)


def cache_kernel(
    group, count_up, len_ref, tick_ref, q_hbm, kv_hbm, *refs
):
    up_refs, refs = refs[:count_up], refs[count_up:]
    q_out, acc_out, top_out, sum_out, up_out, q_ref, kv_ref, sems = refs
    held = up_refs[0].shape[1]
    for i, up_ref in enumerate(up_refs):
        up_out[:, i * held : (i + 1) * held] = up_ref[...]
    copies = [
        pltpu.make_async_copy(q_hbm, q_ref, sems.at[0]),
        pltpu.make_async_copy(kv_hbm.at[0], kv_ref.at[0], sems.at[1]),
        pltpu.make_async_copy(kv_hbm.at[1], kv_ref.at[1], sems.at[2]),
    ]
    for copy in copies:
        copy.start()
    for copy in copies:
        copy.wait()
    rows, steps, width = q_ref.shape
    heads, cached = width // (group * HD), kv_ref.shape[2]
    tokens = rows * steps
    flat = jnp.concatenate([q_ref[b].astype(jnp.float32) for b in range(rows)], axis=0)
    flat = flat.astype(jnp.bfloat16)
    count = group * tokens
    row_of = (lax.broadcasted_iota(jnp.int32, (count, 1), 0) % tokens) // steps
    filled = jnp.zeros((count, 1), jnp.int32)
    for b in range(rows):
        filled = jnp.where(row_of == b, len_ref[b], filled)
    position = lax.broadcasted_iota(jnp.int32, (count, cached), 1)
    for g in range(heads):
        query = jnp.concatenate(
            [flat[:, (g * group + h) * HD : (g * group + h + 1) * HD] for h in range(group)], axis=0
        )
        q_out[g] = query
        cols = slice(g * HD, (g + 1) * HD)
        scores = []
        for b in range(rows):
            valid = jnp.logical_and(row_of == b, position < filled)
            scores.append(jnp.where(valid, dot(query, kv_ref[0, b, :, cols], NT) * HD**-0.5, NEG))
        top = functools.reduce(jnp.maximum, [jnp.max(x, axis=1, keepdims=True) for x in scores])
        total = jnp.zeros((count, 1), jnp.float32)
        mixed = jnp.zeros((count, HD), jnp.float32)
        for b in range(rows):
            weight = jnp.exp(scores[b] - top)
            total = total + jnp.sum(weight, axis=1, keepdims=True)
            high = weight.astype(jnp.bfloat16)
            low = (weight - high.astype(jnp.float32)).astype(jnp.bfloat16)
            values = kv_ref[1, b, :, cols]
            mixed = mixed + dot(high, values) + dot(low, values)
        acc_out[g] = mixed
        top_out[g] = jnp.broadcast_to(top, (count, HD))
        sum_out[g] = jnp.broadcast_to(total, (count, HD))


def early_kernel(blocks, chunk, sizes, items, base_hbm, *refs):
    x_refs, refs = refs[:blocks], refs[blocks:]
    if blocks == 2:
        x_refs, refs = x_refs + refs[:1], refs[1:]
    a_refs, (out_ref, x_out, base_ref, sems) = refs[:-4], refs[-4:]
    columns, slab, ranks = base_hbm.shape[2], a_refs[0].shape[2], a_refs[0].shape[1]
    rows, steps, wide = x_refs[0].shape
    block = lax.div(lax.axis_index("fsdp"), sizes[0] // sizes[1])
    place = places(sizes, items)
    first = pl.multiple_of(block * wide, wide)
    copies = []
    for i in range(wide // chunk):
        for m in range(2):
            copies.append(
                pltpu.make_async_copy(
                    base_hbm.at[m, pl.ds(first + i * chunk, chunk)],
                    base_ref.at[m, pl.ds(i * chunk, chunk)],
                    sems.at[2 * i + m],
                )
            )
    for copy in copies:
        copy.start()
    moved = lax.axis_index("tp") != block
    for k in range(blocks):
        pieces = []
        for b in range(rows):
            x = x_refs[k][b].astype(jnp.float32)
            if len(x_refs) > blocks:
                x = jnp.where(moved, x_refs[k + 1][b].astype(jnp.float32), x)
            pieces.append(x)
        x = jnp.concatenate(pieces, axis=0)
        x_out[k * rows * steps : (k + 1) * rows * steps] = x.astype(jnp.bfloat16)
    count = blocks * rows * steps
    total = jnp.zeros((count, 2 * ranks), jnp.float32)
    for i, a in enumerate(a_refs):
        start = pl.multiple_of(place[i] * slab, slab)
        total = total + dot(x_out[:, pl.ds(start, slab)], a[...].reshape(2 * ranks, slab), NT)
    out_ref[:, 2 * columns :] = total
    totals = [jnp.zeros((count, columns), jnp.float32) for _ in range(2)]
    for i in range(wide // chunk):
        at = slice(i * chunk, (i + 1) * chunk)
        for m in range(2):
            copies[2 * i + m].wait()
            totals[m] = totals[m] + dot(x_out[:, at], base_ref[m, at])
    for m in range(2):
        out_ref[:, m * columns : (m + 1) * columns] = totals[m]


def late_kernel(blocks, columns, sizes, items, part_ref, x_ref, *refs):
    a_refs, outs = refs[:-blocks], refs[-blocks:]
    tokens = outs[0].shape[0]
    slab, ranks = a_refs[0].shape[2], a_refs[0].shape[1]
    place = places(sizes, items)
    total = part_ref[:, 2 * columns :]
    for i, a in enumerate(a_refs):
        start = pl.multiple_of(place[i] * slab, slab)
        total = total + dot(x_ref[:, pl.ds(start, slab)], a[...].reshape(2 * ranks, slab), NT)
    for j, out in enumerate(outs):
        at = slice(j * tokens, (j + 1) * tokens)
        out[:, : 2 * columns] = part_ref[at, : 2 * columns].astype(out.dtype)
        out[:, 2 * columns :] = total[at].astype(out.dtype)


def tick_kernel(out_ref):
    out_ref[...] = jnp.zeros(out_ref.shape, jnp.float32)


def collect_kernel(*refs):
    rows = refs[0].shape[1]
    for k, ref in enumerate(refs[:-1]):
        refs[-1][:, k * rows : (k + 1) * rows] = ref[...]


def order_kernel(count, cores, *refs):
    out = refs[-1]
    f, s = lax.axis_index("fsdp"), lax.axis_index("sub")
    rows = refs[0].shape[1] // count
    for i, ref in enumerate(refs[:-1]):
        for k in range(count):
            start = pl.multiple_of(((f ^ k) * cores + (s ^ i)) * rows, rows)
            out[:, pl.ds(start, rows)] = ref[:, k * rows : (k + 1) * rows]


def rank_kernel(columns, mine_ref, *refs):
    total = mine_ref[:, 2 * columns :]
    for other in refs[:-1]:
        total = total + other[:, 2 * columns :].astype(jnp.float32)
    refs[-1][...] = total.astype(jnp.bfloat16)


def first_kernel(blocks, mine_ref, *refs):
    others, (rank_ref, up_ref, out_ref) = refs[: blocks - 1], refs[blocks - 1 :]
    columns, ranks = up_ref.shape[2], rank_ref.shape[1] // 2
    start = pl.multiple_of(lax.axis_index("tp") * ranks, ranks)
    for m in range(2):
        cols = slice(m * columns, (m + 1) * columns)
        total = mine_ref[:, cols]
        for other in others:
            total = total + other[:, cols].astype(jnp.float32)
        rank = rank_ref[:, m * ranks : (m + 1) * ranks]
        out_ref[:, cols] = total + dot(rank, up_ref[m, pl.ds(start, ranks)])


def final_kernel(blocks, steps, group, sum_in, *refs):
    rank_refs, refs = refs[: blocks - 1], refs[blocks - 1 :]
    up_ref, q_ref, acc_ref, top_ref, sum_ref, fresh_out, out = refs
    tokens, columns = sum_in.shape[0], fresh_out.shape[3]
    rows, heads = tokens // steps, columns // HD
    ranks = rank_refs[0].shape[1] // 2
    fresh = []
    for m in range(2):
        total = sum_in[:, m * columns : (m + 1) * columns]
        for i, rank in enumerate(rank_refs):
            other = lax.rem(lax.axis_index("tp") - (i + 1) + blocks, blocks)
            start = pl.multiple_of(other * ranks, ranks)
            total = total + dot(rank[:, m * ranks : (m + 1) * ranks], up_ref[m, pl.ds(start, ranks)])
        for b in range(rows):
            fresh_out[m, b] = total[b * steps : (b + 1) * steps].astype(jnp.bfloat16)
        fresh.append(total.astype(jnp.bfloat16))
    count = group * tokens
    token = lax.broadcasted_iota(jnp.int32, (count, tokens), 0) % tokens
    key = lax.broadcasted_iota(jnp.int32, (count, tokens), 1)
    valid = jnp.logical_and(token // steps == key // steps, key <= token)
    for g in range(heads):
        cols = slice(g * HD, (g + 1) * HD)
        scores = jnp.where(valid, dot(q_ref[g], fresh[0][:, cols], NT) * HD**-0.5, NEG)
        top_old = top_ref[g][:, :1]
        top = jnp.maximum(top_old, jnp.max(scores, axis=1, keepdims=True))
        scale = jnp.exp(top_old - top)
        weight = jnp.where(valid, jnp.exp(scores - top), 0.0)
        total = sum_ref[g][:, :1] * scale + jnp.sum(weight, axis=1, keepdims=True)
        weight = (weight / total).astype(jnp.bfloat16)
        mixed = acc_ref[g] * (scale / total) + dot(weight, fresh[1][:, cols])
        for h in range(group):
            lanes = slice((g * group + h) * HD, (g * group + h + 1) * HD)
            for b in range(rows):
                at = h * tokens + b * steps
                out[b, :, lanes] = mixed[at : at + steps].astype(jnp.bfloat16)


def smem():
    return pl.BlockSpec(memory_space=pltpu.SMEM)


def local(sizes, inputs, queries, kv_cache, lengths, base, a_factor, b_factor):
    fsdp, tp, sub = sizes
    inner = fsdp // tp
    row_count, steps, wide = inputs.shape
    tokens, columns, ranks = row_count * steps, base.shape[2], a_factor.shape[1]
    heads, group = columns // HD, QH // KVH
    f, t, s = lax.axis_index("fsdp"), lax.axis_index("tp"), lax.axis_index("sub")
    p, r = f // inner, f % inner
    bf16, f32 = jnp.bfloat16, jnp.float32

    def over_fsdp(x, k):
        return lax.ppermute(x, "fsdp", [(i, i ^ k) for i in range(fsdp)])

    def over_sub(x, k):
        return lax.ppermute(x, "sub", [(i, i ^ k) for i in range(sub)])

    def spread(x, k):
        pairs = []
        for i in range(fsdp):
            for j in range(tp):
                pairs.append((i * tp + j, (j * inner + i % inner) * tp + (i // inner + k) % tp))
        return lax.ppermute(x, ("fsdp", "tp"), pairs)

    xs = [spread(inputs, k) for k in range(1 if tp == 2 else 0, tp)]

    tick = pl.pallas_call(
        tick_kernel,
        out_shape=jax.ShapeDtypeStruct((8, 128), f32),
        out_specs=vmem(),
        cost_estimate=cost(8.0),
        name="tick",
    )()

    a_own, tick = lax.optimization_barrier((a_factor, tick))
    far = [over_fsdp(a_own, k) for k in range(1, inner)]
    near = [(0, e, over_sub(a_factor, e)) for e in range(1, sub)]

    def join(mine, other, bit):
        low = jnp.where(bit == 0, mine, other)
        high = jnp.where(bit == 0, other, mine)
        return jnp.concatenate([low, high], axis=1)

    def gather(x, axis, index, start, stop):
        size = {"fsdp": fsdp, "sub": sub}[axis]
        while start < stop:
            other = lax.ppermute(x, axis, [(i, i ^ start) for i in range(size)])
            x = join(x, other, (index // start) % 2)
            start = start * 2
        return x

    up = b_factor.transpose(0, 2, 1)
    direct = fsdp == 4 and inner == 2 and up.shape[1] % 16 == 0
    if direct:
        up = [up, over_fsdp(up, 1)]
    else:
        up = gather(gather(up[:, None], "fsdp", f, 1, fsdp), "sub", s, 1, sub)
        up = [up.reshape(2, sub, fsdp, -1, columns).swapaxes(1, 2).reshape(2, -1, columns)]

    count = group * tokens
    per_head = jax.ShapeDtypeStruct((heads, count, HD), f32)
    *state, up = pl.pallas_call(
        functools.partial(cache_kernel, group, len(up)),
        out_shape=[
            jax.ShapeDtypeStruct((heads, count, HD), bf16),
            per_head,
            per_head,
            per_head,
            jax.ShapeDtypeStruct((2, len(up) * up[0].shape[1], columns), bf16),
        ],
        in_specs=[smem(), vmem()] + [pl.BlockSpec(memory_space=pltpu.HBM)] * 2 + [vmem()] * len(up),
        out_specs=[vmem()] * 5,
        scratch_shapes=[
            pltpu.VMEM(queries.shape, bf16),
            pltpu.VMEM(kv_cache.shape, bf16),
            pltpu.SemaphoreType.DMA((3,)),
        ],
        compiler_params=params(40),
        cost_estimate=cost(C_CACHED),
        name="cached",
    )(lengths, tick, queries, kv_cache, *up)

    xs, near_a = lax.optimization_barrier((xs, up))
    if tp == 2:
        pairs = [(i * tp + i // inner, i * tp + 1 - i // inner) for i in range(fsdp)]
        xs = [inputs, xs[0], lax.ppermute(xs[0], ("fsdp", "tp"), pairs)]
    else:
        xs = jnp.stack(xs)
        xs = [lax.dynamic_index_in_dim(xs, (t - p - j) % tp, keepdims=False) for j in range(tp)]
    near = [(0, 0, a_factor)] + near
    up = [up, over_fsdp(up, inner)] if direct else [up]
    width = 2 * columns + 2 * ranks
    part, x = pl.pallas_call(
        functools.partial(early_kernel, tp, wide // 4, sizes, [(k, e) for k, e, _ in near]),
        out_shape=[
            jax.ShapeDtypeStruct((tp * tokens, width), f32),
            jax.ShapeDtypeStruct((tp * tokens, wide), bf16),
        ],
        in_specs=[pl.BlockSpec(memory_space=pltpu.HBM)] + [vmem()] * (len(xs) + len(near)),
        out_specs=[vmem()] * 2,
        scratch_shapes=[pltpu.VMEM((2, wide, columns), bf16), pltpu.SemaphoreType.DMA((8,))],
        compiler_params=params(50),
        cost_estimate=cost(C_EARLY),
        name="early",
    )(base, *xs, *[a for _, _, a in near])

    far, part, up = lax.optimization_barrier((far, part, up))
    late_at = [(k, e) for k in range(1, inner) for e in range(sub)]
    late = [over_sub(far[k - 1], e) if e else far[k - 1] for k, e in late_at]
    parts = pl.pallas_call(
        functools.partial(late_kernel, tp, columns, sizes, late_at),
        out_shape=[jax.ShapeDtypeStruct((tokens, width), f32 if j == 0 else bf16) for j in range(tp)],
        in_specs=[vmem()] * (2 + len(late)),
        out_specs=[vmem()] * tp,
        compiler_params=params(),
        name="late",
    )(part, x, *late)

    parts, up = lax.optimization_barrier((parts, up))
    others = []
    for j in range(1, tp):
        pairs = [(i, (i + j * inner) % fsdp) for i in range(fsdp)]
        others.append(lax.ppermute(parts[j], "fsdp", pairs))

    if direct:
        rows_up = up[0].shape[1] * 2
        mine = pl.pallas_call(
            collect_kernel,
            out_shape=jax.ShapeDtypeStruct((2, rows_up, columns), bf16),
            in_specs=[vmem()] * 2,
            out_specs=vmem(),
            compiler_params=params(),
            name="collect",
        )(*up)
        up = [mine] + [over_sub(mine, e) for e in range(1, sub)]
        up = pl.pallas_call(
            functools.partial(order_kernel, fsdp, sub),
            out_shape=jax.ShapeDtypeStruct((2, sub * rows_up, columns), bf16),
            in_specs=[vmem()] * sub,
            out_specs=vmem(),
            compiler_params=params(),
        cost_estimate=cost(1.0),
            name="order",
        )(*up)
    else:
        up = up[0]

    own = pl.pallas_call(
        functools.partial(rank_kernel, columns),
        out_shape=jax.ShapeDtypeStruct((tokens, 2 * ranks), bf16),
        in_specs=[vmem()] * tp,
        out_specs=vmem(),
        compiler_params=params(),
        cost_estimate=cost(4.0),
        name="ranks",
    )(parts[0], *others)
    rank_parts = [own]
    for i in range(1, tp):
        rank_parts.append(lax.ppermute(own, "tp", [(j, (j + i) % tp) for j in range(tp)]))

    first = pl.pallas_call(
        functools.partial(first_kernel, tp),
        out_shape=jax.ShapeDtypeStruct((tokens, 2 * columns), f32),
        in_specs=[vmem()] * (tp + 2),
        out_specs=vmem(),
        compiler_params=params(),
        name="first",
    )(parts[0], *others, own, up)
    fresh, attended = pl.pallas_call(
        functools.partial(final_kernel, tp, steps, group),
        out_shape=(
            jax.ShapeDtypeStruct((2, row_count, steps, columns), bf16),
            jax.ShapeDtypeStruct(queries.shape, bf16),
        ),
        in_specs=[vmem()] * (tp + 5),
        out_specs=[vmem(), vmem()],
        compiler_params=params(),
        name="final",
    )(first, *rank_parts[1:], up, *state)
    return fresh, attended


def solution(mesh):
    sizes = tuple(mesh.shape[axis] for axis in ("fsdp", "tp", "sub"))
    return jax.shard_map(
        functools.partial(local, sizes),
        mesh=mesh,
        in_specs=(
            P(("groups", "fsdp", "sub"), None, "tp"),
            P(("groups", "fsdp", "sub"), None, "tp"),
            P(None, ("groups", "fsdp", "sub"), None, "tp"),
            P(("groups", "fsdp", "sub")),
            P(None, None, "tp"),
            P(None, "tp", ("fsdp", "sub")),
            P(None, "tp", ("fsdp", "sub")),
        ),
        out_specs=(
            P(None, ("groups", "fsdp", "sub"), None, "tp"),
            P(("groups", "fsdp", "sub"), None, "tp"),
        ),
        check_vma=False,
    )
```

```python
import functools

import jax
import jax.numpy as jnp
from jax import lax
from jax.experimental import pallas as pl
from jax.experimental.pallas import tpu as pltpu
from jax.sharding import PartitionSpec as P

HD = 128
KVH = 4
QH = 32

C_CACHED = 2.0
C_EARLY = 3.0
NEG = -1e30

NT = (((1,), (1,)), ((), ()))
NN = (((1,), (0,)), ((), ()))


def dot(x, y, dims=NN):
    return lax.dot_general(x, y, dims, preferred_element_type=jnp.float32)


def cost(us):
    return pl.CostEstimate(flops=int(us * 1e9), bytes_accessed=int(us * 3e6), transcendentals=0)


def places(sizes, items):
    row, core = lax.rem(lax.axis_index("fsdp"), sizes[0] // sizes[1]), lax.axis_index("sub")
    return [(row ^ k) * sizes[2] + (core ^ e) for k, e in items]


def vmem():
    return pl.BlockSpec(memory_space=pltpu.VMEM)


def params(mib=40):
    return pltpu.CompilerParams(vmem_limit_bytes=mib * 2**20)


def cache_kernel(
    group, count_up, len_ref, tick_ref, q_hbm, kv_hbm, *refs
):
    up_refs, refs = refs[:count_up], refs[count_up:]
    q_out, acc_out, top_out, sum_out, up_out, q_ref, kv_ref, sems = refs
    held = up_refs[0].shape[1]
    for i, up_ref in enumerate(up_refs):
        up_out[:, i * held : (i + 1) * held] = up_ref[...]
    copies = [
        pltpu.make_async_copy(q_hbm, q_ref, sems.at[0]),
        pltpu.make_async_copy(kv_hbm.at[0], kv_ref.at[0], sems.at[1]),
        pltpu.make_async_copy(kv_hbm.at[1], kv_ref.at[1], sems.at[2]),
    ]
    for copy in copies:
        copy.start()
    for copy in copies:
        copy.wait()
    rows, steps, width = q_ref.shape
    heads, cached = width // (group * HD), kv_ref.shape[2]
    tokens = rows * steps
    flat = jnp.concatenate([q_ref[b].astype(jnp.float32) for b in range(rows)], axis=0)
    flat = flat.astype(jnp.bfloat16)
    count = group * tokens
    row_of = (lax.broadcasted_iota(jnp.int32, (count, 1), 0) % tokens) // steps
    filled = jnp.zeros((count, 1), jnp.int32)
    for b in range(rows):
        filled = jnp.where(row_of == b, len_ref[b], filled)
    position = lax.broadcasted_iota(jnp.int32, (count, cached), 1)
    for g in range(heads):
        query = jnp.concatenate(
            [flat[:, (g * group + h) * HD : (g * group + h + 1) * HD] for h in range(group)], axis=0
        )
        q_out[g] = query
        cols = slice(g * HD, (g + 1) * HD)
        scores = []
        for b in range(rows):
            valid = jnp.logical_and(row_of == b, position < filled)
            scores.append(jnp.where(valid, dot(query, kv_ref[0, b, :, cols], NT) * HD**-0.5, NEG))
        top = functools.reduce(jnp.maximum, [jnp.max(x, axis=1, keepdims=True) for x in scores])
        total = jnp.zeros((count, 1), jnp.float32)
        mixed = jnp.zeros((count, HD), jnp.float32)
        for b in range(rows):
            weight = jnp.exp(scores[b] - top)
            total = total + jnp.sum(weight, axis=1, keepdims=True)
            high = weight.astype(jnp.bfloat16)
            low = (weight - high.astype(jnp.float32)).astype(jnp.bfloat16)
            values = kv_ref[1, b, :, cols]
            mixed = mixed + dot(high, values) + dot(low, values)
        acc_out[g] = mixed
        top_out[g] = jnp.broadcast_to(top, (count, HD))
        sum_out[g] = jnp.broadcast_to(total, (count, HD))


def early_kernel(blocks, chunk, sizes, items, base_hbm, *refs):
    x_refs, refs = refs[:blocks], refs[blocks:]
    if blocks == 2:
        x_refs, refs = x_refs + refs[:1], refs[1:]
    a_refs, refs = refs[: len(items)], refs[len(items) :]
    out_ref, x_out, *send_outs, base_ref, sems = refs
    columns, slab, ranks = base_hbm.shape[2], a_refs[0].shape[2], a_refs[0].shape[1]
    rows, steps, wide = x_refs[0].shape
    block = lax.div(lax.axis_index("fsdp"), sizes[0] // sizes[1])
    place = places(sizes, items)
    first = pl.multiple_of(block * wide, wide)
    copies = []
    for i in range(wide // chunk):
        for m in range(2):
            copies.append(
                pltpu.make_async_copy(
                    base_hbm.at[m, pl.ds(first + i * chunk, chunk)],
                    base_ref.at[m, pl.ds(i * chunk, chunk)],
                    sems.at[2 * i + m],
                )
            )
    for copy in copies:
        copy.start()
    moved = lax.axis_index("tp") != block
    for k in range(blocks):
        pieces = []
        for b in range(rows):
            x = x_refs[k][b].astype(jnp.float32)
            if len(x_refs) > blocks:
                x = jnp.where(moved, x_refs[k + 1][b].astype(jnp.float32), x)
            pieces.append(x)
        x = jnp.concatenate(pieces, axis=0)
        x_out[k * rows * steps : (k + 1) * rows * steps] = x.astype(jnp.bfloat16)
    count = blocks * rows * steps
    total = jnp.zeros((count, 2 * ranks), jnp.float32)
    for i, a in enumerate(a_refs):
        start = pl.multiple_of(place[i] * slab, slab)
        total = total + dot(x_out[:, pl.ds(start, slab)], a[...].reshape(2 * ranks, slab), NT)
    out_ref[:, 2 * columns :] = total
    for place_to, send in zip(places(sizes, [(k + 1, 1) for k in range(len(send_outs))]), send_outs):
        send[...] = x_out[:, pl.ds(pl.multiple_of(place_to * slab, slab), slab)]
    totals = [jnp.zeros((count, columns), jnp.float32) for _ in range(2)]
    for i in range(wide // chunk):
        at = slice(i * chunk, (i + 1) * chunk)
        for m in range(2):
            copies[2 * i + m].wait()
            totals[m] = totals[m] + dot(x_out[:, at], base_ref[m, at])
    for m in range(2):
        out_ref[:, m * columns : (m + 1) * columns] = totals[m]


def far_kernel(sizes, count, part_ref, x_ref, *refs):
    other_refs, a_refs, (own_out, other_out) = refs[:count], refs[count:-2], refs[-2:]
    slab, ranks = a_refs[0].shape[2], a_refs[0].shape[1]
    columns = part_ref.shape[1] - 2 * ranks
    place = places(sizes, [(k + 1, 0) for k in range(count)])
    own = part_ref[:, columns:]
    other = jnp.zeros(own.shape, jnp.float32)
    for k, a in enumerate(a_refs):
        factor = a[...].reshape(2 * ranks, slab)
        start = pl.multiple_of(place[k] * slab, slab)
        own = own + dot(x_ref[:, pl.ds(start, slab)], factor, NT)
        other = other + dot(other_refs[k][...], factor, NT)
    own_out[...] = own
    other_out[...] = other.astype(jnp.bfloat16)


def late_kernel(columns, part_ref, own_ref, other_ref, *outs):
    tokens = outs[0].shape[0]
    total = own_ref[...] + other_ref[...].astype(jnp.float32)
    for j, out in enumerate(outs):
        at = slice(j * tokens, (j + 1) * tokens)
        out[:, : 2 * columns] = part_ref[at, : 2 * columns].astype(out.dtype)
        out[:, 2 * columns :] = total[at].astype(out.dtype)


def tick_kernel(out_ref):
    out_ref[...] = jnp.zeros(out_ref.shape, jnp.float32)


def collect_kernel(*refs):
    rows = refs[0].shape[1]
    for k, ref in enumerate(refs[:-1]):
        refs[-1][:, k * rows : (k + 1) * rows] = ref[...]


def order_kernel(count, cores, *refs):
    out = refs[-1]
    f, s = lax.axis_index("fsdp"), lax.axis_index("sub")
    rows = refs[0].shape[1] // count
    for i, ref in enumerate(refs[:-1]):
        for k in range(count):
            start = pl.multiple_of(((f ^ k) * cores + (s ^ i)) * rows, rows)
            out[:, pl.ds(start, rows)] = ref[:, k * rows : (k + 1) * rows]


def rank_kernel(columns, mine_ref, *refs):
    total = mine_ref[:, 2 * columns :]
    for other in refs[:-1]:
        total = total + other[:, 2 * columns :].astype(jnp.float32)
    refs[-1][...] = total.astype(jnp.bfloat16)


def first_kernel(blocks, mine_ref, *refs):
    others, (rank_ref, up_ref, out_ref) = refs[: blocks - 1], refs[blocks - 1 :]
    columns, ranks = up_ref.shape[2], rank_ref.shape[1] // 2
    start = pl.multiple_of(lax.axis_index("tp") * ranks, ranks)
    for m in range(2):
        cols = slice(m * columns, (m + 1) * columns)
        total = mine_ref[:, cols]
        for other in others:
            total = total + other[:, cols].astype(jnp.float32)
        rank = rank_ref[:, m * ranks : (m + 1) * ranks]
        out_ref[:, cols] = total + dot(rank, up_ref[m, pl.ds(start, ranks)])


def final_kernel(blocks, steps, group, sum_in, *refs):
    rank_refs, refs = refs[: blocks - 1], refs[blocks - 1 :]
    up_ref, q_ref, acc_ref, top_ref, sum_ref, fresh_out, out = refs
    tokens, columns = sum_in.shape[0], fresh_out.shape[3]
    rows, heads = tokens // steps, columns // HD
    ranks = rank_refs[0].shape[1] // 2
    fresh = []
    for m in range(2):
        total = sum_in[:, m * columns : (m + 1) * columns]
        for i, rank in enumerate(rank_refs):
            other = lax.rem(lax.axis_index("tp") - (i + 1) + blocks, blocks)
            start = pl.multiple_of(other * ranks, ranks)
            total = total + dot(rank[:, m * ranks : (m + 1) * ranks], up_ref[m, pl.ds(start, ranks)])
        for b in range(rows):
            fresh_out[m, b] = total[b * steps : (b + 1) * steps].astype(jnp.bfloat16)
        fresh.append(total.astype(jnp.bfloat16))
    count = group * tokens
    token = lax.broadcasted_iota(jnp.int32, (count, tokens), 0) % tokens
    key = lax.broadcasted_iota(jnp.int32, (count, tokens), 1)
    valid = jnp.logical_and(token // steps == key // steps, key <= token)
    for g in range(heads):
        cols = slice(g * HD, (g + 1) * HD)
        scores = jnp.where(valid, dot(q_ref[g], fresh[0][:, cols], NT) * HD**-0.5, NEG)
        top_old = top_ref[g][:, :1]
        top = jnp.maximum(top_old, jnp.max(scores, axis=1, keepdims=True))
        scale = jnp.exp(top_old - top)
        weight = jnp.where(valid, jnp.exp(scores - top), 0.0)
        total = sum_ref[g][:, :1] * scale + jnp.sum(weight, axis=1, keepdims=True)
        weight = (weight / total).astype(jnp.bfloat16)
        mixed = acc_ref[g] * (scale / total) + dot(weight, fresh[1][:, cols])
        for h in range(group):
            lanes = slice((g * group + h) * HD, (g * group + h + 1) * HD)
            for b in range(rows):
                at = h * tokens + b * steps
                out[b, :, lanes] = mixed[at : at + steps].astype(jnp.bfloat16)


def smem():
    return pl.BlockSpec(memory_space=pltpu.SMEM)


def local(sizes, inputs, queries, kv_cache, lengths, base, a_factor, b_factor):
    fsdp, tp, sub = sizes
    inner = fsdp // tp
    row_count, steps, wide = inputs.shape
    tokens, columns, ranks = row_count * steps, base.shape[2], a_factor.shape[1]
    heads, group = columns // HD, QH // KVH
    f, t, s = lax.axis_index("fsdp"), lax.axis_index("tp"), lax.axis_index("sub")
    p, r = f // inner, f % inner
    bf16, f32 = jnp.bfloat16, jnp.float32

    def over_fsdp(x, k):
        return lax.ppermute(x, "fsdp", [(i, i ^ k) for i in range(fsdp)])

    def over_sub(x, k):
        return lax.ppermute(x, "sub", [(i, i ^ k) for i in range(sub)])

    def spread(x, k):
        pairs = []
        for i in range(fsdp):
            for j in range(tp):
                pairs.append((i * tp + j, (j * inner + i % inner) * tp + (i // inner + k) % tp))
        return lax.ppermute(x, ("fsdp", "tp"), pairs)

    xs = [spread(inputs, k) for k in range(1 if tp == 2 else 0, tp)]

    tick = pl.pallas_call(
        tick_kernel,
        out_shape=jax.ShapeDtypeStruct((8, 128), f32),
        out_specs=vmem(),
        cost_estimate=cost(8.0),
        name="tick",
    )()

    a_own, tick = lax.optimization_barrier((a_factor, tick))
    far = [over_fsdp(a_own, k) for k in range(1, inner)]
    near = [(0, e, over_sub(a_factor, e)) for e in range(1, sub)]

    def join(mine, other, bit):
        low = jnp.where(bit == 0, mine, other)
        high = jnp.where(bit == 0, other, mine)
        return jnp.concatenate([low, high], axis=1)

    def gather(x, axis, index, start, stop):
        size = {"fsdp": fsdp, "sub": sub}[axis]
        while start < stop:
            other = lax.ppermute(x, axis, [(i, i ^ start) for i in range(size)])
            x = join(x, other, (index // start) % 2)
            start = start * 2
        return x

    up = b_factor.transpose(0, 2, 1)
    direct = fsdp == 4 and inner == 2 and up.shape[1] % 16 == 0
    if direct:
        up = [up, over_fsdp(up, 1)]
    else:
        up = gather(gather(up[:, None], "fsdp", f, 1, fsdp), "sub", s, 1, sub)
        up = [up.reshape(2, sub, fsdp, -1, columns).swapaxes(1, 2).reshape(2, -1, columns)]

    count = group * tokens
    per_head = jax.ShapeDtypeStruct((heads, count, HD), f32)
    *state, up = pl.pallas_call(
        functools.partial(cache_kernel, group, len(up)),
        out_shape=[
            jax.ShapeDtypeStruct((heads, count, HD), bf16),
            per_head,
            per_head,
            per_head,
            jax.ShapeDtypeStruct((2, len(up) * up[0].shape[1], columns), bf16),
        ],
        in_specs=[smem(), vmem()] + [pl.BlockSpec(memory_space=pltpu.HBM)] * 2 + [vmem()] * len(up),
        out_specs=[vmem()] * 5,
        scratch_shapes=[
            pltpu.VMEM(queries.shape, bf16),
            pltpu.VMEM(kv_cache.shape, bf16),
            pltpu.SemaphoreType.DMA((3,)),
        ],
        compiler_params=params(40),
        cost_estimate=cost(C_CACHED),
        name="cached",
    )(lengths, tick, queries, kv_cache, *up)

    xs, near_a = lax.optimization_barrier((xs, up))
    if tp == 2:
        pairs = [(i * tp + i // inner, i * tp + 1 - i // inner) for i in range(fsdp)]
        xs = [inputs, xs[0], lax.ppermute(xs[0], ("fsdp", "tp"), pairs)]
    else:
        xs = jnp.stack(xs)
        xs = [lax.dynamic_index_in_dim(xs, (t - p - j) % tp, keepdims=False) for j in range(tp)]
    near = [(0, 0, a_factor)] + near
    up = [up, over_fsdp(up, inner)] if direct else [up]
    width = 2 * columns + 2 * ranks
    part, x, *x_sends = pl.pallas_call(
        functools.partial(early_kernel, tp, wide // 4, sizes, [(k, e) for k, e, _ in near]),
        out_shape=[
            jax.ShapeDtypeStruct((tp * tokens, width), f32),
            jax.ShapeDtypeStruct((tp * tokens, wide), bf16),
        ]
        + [jax.ShapeDtypeStruct((tp * tokens, a_factor.shape[2]), bf16)] * (inner - 1),
        in_specs=[pl.BlockSpec(memory_space=pltpu.HBM)] + [vmem()] * (len(xs) + len(near)),
        out_specs=[vmem()] * (1 + inner),
        scratch_shapes=[pltpu.VMEM((2, wide, columns), bf16), pltpu.SemaphoreType.DMA((8,))],
        compiler_params=params(50),
        cost_estimate=cost(C_EARLY),
        name="early",
    )(base, *xs, *[a for _, _, a in near])

    x_others = [over_sub(x, 1) for x in x_sends]
    far, part, up, x_others = lax.optimization_barrier((far, part, up, x_others))
    far_own, far_other = pl.pallas_call(
        functools.partial(far_kernel, sizes, inner - 1),
        out_shape=[
            jax.ShapeDtypeStruct((tp * tokens, 2 * ranks), f32),
            jax.ShapeDtypeStruct((tp * tokens, 2 * ranks), bf16),
        ],
        in_specs=[vmem()] * (2 * inner),
        out_specs=[vmem()] * 2,
        compiler_params=params(),
        name="far",
    )(part, x, *x_others, *far)
    parts = pl.pallas_call(
        functools.partial(late_kernel, columns),
        out_shape=[jax.ShapeDtypeStruct((tokens, width), f32 if j == 0 else bf16) for j in range(tp)],
        in_specs=[vmem()] * 3,
        out_specs=[vmem()] * tp,
        compiler_params=params(),
        name="late",
    )(part, far_own, over_sub(far_other, 1))

    parts, up = lax.optimization_barrier((parts, up))
    others = []
    for j in range(1, tp):
        pairs = [(i, (i + j * inner) % fsdp) for i in range(fsdp)]
        others.append(lax.ppermute(parts[j], "fsdp", pairs))

    if direct:
        rows_up = up[0].shape[1] * 2
        mine = pl.pallas_call(
            collect_kernel,
            out_shape=jax.ShapeDtypeStruct((2, rows_up, columns), bf16),
            in_specs=[vmem()] * 2,
            out_specs=vmem(),
            compiler_params=params(),
            name="collect",
        )(*up)
        up = [mine] + [over_sub(mine, e) for e in range(1, sub)]
        up = pl.pallas_call(
            functools.partial(order_kernel, fsdp, sub),
            out_shape=jax.ShapeDtypeStruct((2, sub * rows_up, columns), bf16),
            in_specs=[vmem()] * sub,
            out_specs=vmem(),
            compiler_params=params(),
        cost_estimate=cost(1.0),
            name="order",
        )(*up)
    else:
        up = up[0]

    own = pl.pallas_call(
        functools.partial(rank_kernel, columns),
        out_shape=jax.ShapeDtypeStruct((tokens, 2 * ranks), bf16),
        in_specs=[vmem()] * tp,
        out_specs=vmem(),
        compiler_params=params(),
        cost_estimate=cost(4.0),
        name="ranks",
    )(parts[0], *others)
    rank_parts = [own]
    for i in range(1, tp):
        rank_parts.append(lax.ppermute(own, "tp", [(j, (j + i) % tp) for j in range(tp)]))

    first = pl.pallas_call(
        functools.partial(first_kernel, tp),
        out_shape=jax.ShapeDtypeStruct((tokens, 2 * columns), f32),
        in_specs=[vmem()] * (tp + 2),
        out_specs=vmem(),
        compiler_params=params(),
        name="first",
    )(parts[0], *others, own, up)
    fresh, attended = pl.pallas_call(
        functools.partial(final_kernel, tp, steps, group),
        out_shape=(
            jax.ShapeDtypeStruct((2, row_count, steps, columns), bf16),
            jax.ShapeDtypeStruct(queries.shape, bf16),
        ),
        in_specs=[vmem()] * (tp + 5),
        out_specs=[vmem(), vmem()],
        compiler_params=params(),
        name="final",
    )(first, *rank_parts[1:], up, *state)
    return fresh, attended


def solution(mesh):
    sizes = tuple(mesh.shape[axis] for axis in ("fsdp", "tp", "sub"))
    return jax.shard_map(
        functools.partial(local, sizes),
        mesh=mesh,
        in_specs=(
            P(("groups", "fsdp", "sub"), None, "tp"),
            P(("groups", "fsdp", "sub"), None, "tp"),
            P(None, ("groups", "fsdp", "sub"), None, "tp"),
            P(("groups", "fsdp", "sub")),
            P(None, None, "tp"),
            P(None, "tp", ("fsdp", "sub")),
            P(None, "tp", ("fsdp", "sub")),
        ),
        out_specs=(
            P(None, ("groups", "fsdp", "sub"), None, "tp"),
            P(("groups", "fsdp", "sub"), None, "tp"),
        ),
        check_vma=False,
    )
```

```python
import functools

import jax
import jax.numpy as jnp
from jax import lax
from jax.experimental import pallas as pl
from jax.experimental.pallas import tpu as pltpu
from jax.sharding import PartitionSpec as P

HD = 128
KVH = 4
QH = 32

C_CACHED = 2.0
C_EARLY = 3.0
NEG = -1e30

NT = (((1,), (1,)), ((), ()))
NN = (((1,), (0,)), ((), ()))


def dot(x, y, dims=NN):
    return lax.dot_general(x, y, dims, preferred_element_type=jnp.float32)


def cost(us):
    return pl.CostEstimate(flops=int(us * 1e9), bytes_accessed=int(us * 3e6), transcendentals=0)


def places(sizes, items):
    row, core = lax.rem(lax.axis_index("fsdp"), sizes[0] // sizes[1]), lax.axis_index("sub")
    return [(row ^ k) * sizes[2] + (core ^ e) for k, e in items]


def vmem():
    return pl.BlockSpec(memory_space=pltpu.VMEM)


def params(mib=40):
    return pltpu.CompilerParams(vmem_limit_bytes=mib * 2**20)


def cache_kernel(
    group, count_up, len_ref, tick_ref, q_hbm, kv_hbm, *refs
):
    up_refs, refs = refs[:count_up], refs[count_up:]
    q_out, acc_out, top_out, sum_out, up_out, q_ref, kv_ref, sems = refs
    held = up_refs[0].shape[1]
    for i, up_ref in enumerate(up_refs):
        up_out[:, i * held : (i + 1) * held] = up_ref[...]
    copies = [
        pltpu.make_async_copy(q_hbm, q_ref, sems.at[0]),
        pltpu.make_async_copy(kv_hbm.at[0], kv_ref.at[0], sems.at[1]),
        pltpu.make_async_copy(kv_hbm.at[1], kv_ref.at[1], sems.at[2]),
    ]
    for copy in copies:
        copy.start()
    for copy in copies:
        copy.wait()
    rows, steps, width = q_ref.shape
    heads, cached = width // (group * HD), kv_ref.shape[2]
    tokens = rows * steps
    flat = jnp.concatenate([q_ref[b].astype(jnp.float32) for b in range(rows)], axis=0)
    flat = flat.astype(jnp.bfloat16)
    count = group * tokens
    row_of = (lax.broadcasted_iota(jnp.int32, (count, 1), 0) % tokens) // steps
    filled = jnp.zeros((count, 1), jnp.int32)
    for b in range(rows):
        filled = jnp.where(row_of == b, len_ref[b], filled)
    position = lax.broadcasted_iota(jnp.int32, (count, cached), 1)
    for g in range(heads):
        query = jnp.concatenate(
            [flat[:, (g * group + h) * HD : (g * group + h + 1) * HD] for h in range(group)], axis=0
        )
        q_out[g] = query
        cols = slice(g * HD, (g + 1) * HD)
        scores = []
        for b in range(rows):
            valid = jnp.logical_and(row_of == b, position < filled)
            scores.append(jnp.where(valid, dot(query, kv_ref[0, b, :, cols], NT) * HD**-0.5, NEG))
        top = functools.reduce(jnp.maximum, [jnp.max(x, axis=1, keepdims=True) for x in scores])
        total = jnp.zeros((count, 1), jnp.float32)
        mixed = jnp.zeros((count, HD), jnp.float32)
        for b in range(rows):
            weight = jnp.exp(scores[b] - top)
            total = total + jnp.sum(weight, axis=1, keepdims=True)
            high = weight.astype(jnp.bfloat16)
            low = (weight - high.astype(jnp.float32)).astype(jnp.bfloat16)
            values = kv_ref[1, b, :, cols]
            mixed = mixed + dot(high, values) + dot(low, values)
        acc_out[g] = mixed
        top_out[g] = jnp.broadcast_to(top, (count, HD))
        sum_out[g] = jnp.broadcast_to(total, (count, HD))


def early_kernel(blocks, chunk, sizes, items, base_hbm, *refs):
    x_refs, refs = refs[:blocks], refs[blocks:]
    if blocks == 2:
        x_refs, refs = x_refs + refs[:1], refs[1:]
    a_refs, refs = refs[: len(items)], refs[len(items) :]
    out_ref, x_out, *send_outs, base_ref, sems = refs
    columns, slab, ranks = base_hbm.shape[2], a_refs[0].shape[2], a_refs[0].shape[1]
    rows, steps, wide = x_refs[0].shape
    block = lax.div(lax.axis_index("fsdp"), sizes[0] // sizes[1])
    place = places(sizes, items)
    first = pl.multiple_of(block * wide, wide)
    copies = []
    for i in range(wide // chunk):
        for m in range(2):
            copies.append(
                pltpu.make_async_copy(
                    base_hbm.at[m, pl.ds(first + i * chunk, chunk)],
                    base_ref.at[m, pl.ds(i * chunk, chunk)],
                    sems.at[2 * i + m],
                )
            )
    for copy in copies:
        copy.start()
    moved = lax.axis_index("tp") != block
    for k in range(blocks):
        pieces = []
        for b in range(rows):
            x = x_refs[k][b].astype(jnp.float32)
            if len(x_refs) > blocks:
                x = jnp.where(moved, x_refs[k + 1][b].astype(jnp.float32), x)
            pieces.append(x)
        x = jnp.concatenate(pieces, axis=0)
        x_out[k * rows * steps : (k + 1) * rows * steps] = x.astype(jnp.bfloat16)
    count = blocks * rows * steps
    total = jnp.zeros((count, 2 * ranks), jnp.float32)
    for i, a in enumerate(a_refs):
        start = pl.multiple_of(place[i] * slab, slab)
        total = total + dot(x_out[:, pl.ds(start, slab)], a[...].reshape(2 * ranks, slab), NT)
    out_ref[:, 2 * columns :] = total
    for place_to, send in zip(places(sizes, [(k, 1) for k in range(len(send_outs))]), send_outs):
        send[...] = x_out[:, pl.ds(pl.multiple_of(place_to * slab, slab), slab)]
    totals = [jnp.zeros((count, columns), jnp.float32) for _ in range(2)]
    for i in range(wide // chunk):
        at = slice(i * chunk, (i + 1) * chunk)
        for m in range(2):
            copies[2 * i + m].wait()
            totals[m] = totals[m] + dot(x_out[:, at], base_ref[m, at])
    for m in range(2):
        out_ref[:, m * columns : (m + 1) * columns] = totals[m]


def far_kernel(sizes, count, part_ref, x_ref, *refs):
    other_refs, a_refs, (own_out, other_out) = refs[:count], refs[count:-2], refs[-2:]
    slab, ranks = a_refs[0].shape[2], a_refs[0].shape[1]
    columns = part_ref.shape[1] - 2 * ranks
    place = places(sizes, [(k, 0) for k in range(count)])
    own = part_ref[:, columns:]
    other = jnp.zeros(own.shape, jnp.float32)
    for k, a in enumerate(a_refs):
        factor = a[...].reshape(2 * ranks, slab)
        other = other + dot(other_refs[k][...], factor, NT)
        if k > 0:
            start = pl.multiple_of(place[k] * slab, slab)
            own = own + dot(x_ref[:, pl.ds(start, slab)], factor, NT)
    own_out[...] = own
    other_out[...] = other.astype(jnp.bfloat16)


def late_kernel(columns, part_ref, own_ref, other_ref, *outs):
    tokens = outs[0].shape[0]
    total = own_ref[...] + other_ref[...].astype(jnp.float32)
    for j, out in enumerate(outs):
        at = slice(j * tokens, (j + 1) * tokens)
        out[:, : 2 * columns] = part_ref[at, : 2 * columns].astype(out.dtype)
        out[:, 2 * columns :] = total[at].astype(out.dtype)


def tick_kernel(out_ref):
    out_ref[...] = jnp.zeros(out_ref.shape, jnp.float32)


def collect_kernel(*refs):
    rows = refs[0].shape[1]
    for k, ref in enumerate(refs[:-1]):
        refs[-1][:, k * rows : (k + 1) * rows] = ref[...]


def order_kernel(count, cores, *refs):
    out = refs[-1]
    f, s = lax.axis_index("fsdp"), lax.axis_index("sub")
    rows = refs[0].shape[1] // count
    for i, ref in enumerate(refs[:-1]):
        for k in range(count):
            start = pl.multiple_of(((f ^ k) * cores + (s ^ i)) * rows, rows)
            out[:, pl.ds(start, rows)] = ref[:, k * rows : (k + 1) * rows]


def rank_kernel(columns, mine_ref, *refs):
    total = mine_ref[:, 2 * columns :]
    for other in refs[:-1]:
        total = total + other[:, 2 * columns :].astype(jnp.float32)
    refs[-1][...] = total.astype(jnp.bfloat16)


def first_kernel(blocks, mine_ref, *refs):
    others, (rank_ref, up_ref, out_ref) = refs[: blocks - 1], refs[blocks - 1 :]
    columns, ranks = up_ref.shape[2], rank_ref.shape[1] // 2
    start = pl.multiple_of(lax.axis_index("tp") * ranks, ranks)
    for m in range(2):
        cols = slice(m * columns, (m + 1) * columns)
        total = mine_ref[:, cols]
        for other in others:
            total = total + other[:, cols].astype(jnp.float32)
        rank = rank_ref[:, m * ranks : (m + 1) * ranks]
        out_ref[:, cols] = total + dot(rank, up_ref[m, pl.ds(start, ranks)])


def final_kernel(blocks, steps, group, sum_in, *refs):
    rank_refs, refs = refs[: blocks - 1], refs[blocks - 1 :]
    up_ref, q_ref, acc_ref, top_ref, sum_ref, fresh_out, out = refs
    tokens, columns = sum_in.shape[0], fresh_out.shape[3]
    rows, heads = tokens // steps, columns // HD
    ranks = rank_refs[0].shape[1] // 2
    fresh = []
    for m in range(2):
        total = sum_in[:, m * columns : (m + 1) * columns]
        for i, rank in enumerate(rank_refs):
            other = lax.rem(lax.axis_index("tp") - (i + 1) + blocks, blocks)
            start = pl.multiple_of(other * ranks, ranks)
            total = total + dot(rank[:, m * ranks : (m + 1) * ranks], up_ref[m, pl.ds(start, ranks)])
        for b in range(rows):
            fresh_out[m, b] = total[b * steps : (b + 1) * steps].astype(jnp.bfloat16)
        fresh.append(total.astype(jnp.bfloat16))
    count = group * tokens
    token = lax.broadcasted_iota(jnp.int32, (count, tokens), 0) % tokens
    key = lax.broadcasted_iota(jnp.int32, (count, tokens), 1)
    valid = jnp.logical_and(token // steps == key // steps, key <= token)
    for g in range(heads):
        cols = slice(g * HD, (g + 1) * HD)
        scores = jnp.where(valid, dot(q_ref[g], fresh[0][:, cols], NT) * HD**-0.5, NEG)
        top_old = top_ref[g][:, :1]
        top = jnp.maximum(top_old, jnp.max(scores, axis=1, keepdims=True))
        scale = jnp.exp(top_old - top)
        weight = jnp.where(valid, jnp.exp(scores - top), 0.0)
        total = sum_ref[g][:, :1] * scale + jnp.sum(weight, axis=1, keepdims=True)
        weight = (weight / total).astype(jnp.bfloat16)
        mixed = acc_ref[g] * (scale / total) + dot(weight, fresh[1][:, cols])
        for h in range(group):
            lanes = slice((g * group + h) * HD, (g * group + h + 1) * HD)
            for b in range(rows):
                at = h * tokens + b * steps
                out[b, :, lanes] = mixed[at : at + steps].astype(jnp.bfloat16)


def smem():
    return pl.BlockSpec(memory_space=pltpu.SMEM)


def local(sizes, inputs, queries, kv_cache, lengths, base, a_factor, b_factor):
    fsdp, tp, sub = sizes
    inner = fsdp // tp
    row_count, steps, wide = inputs.shape
    tokens, columns, ranks = row_count * steps, base.shape[2], a_factor.shape[1]
    heads, group = columns // HD, QH // KVH
    f, t, s = lax.axis_index("fsdp"), lax.axis_index("tp"), lax.axis_index("sub")
    p, r = f // inner, f % inner
    bf16, f32 = jnp.bfloat16, jnp.float32

    def over_fsdp(x, k):
        return lax.ppermute(x, "fsdp", [(i, i ^ k) for i in range(fsdp)])

    def over_sub(x, k):
        return lax.ppermute(x, "sub", [(i, i ^ k) for i in range(sub)])

    def spread(x, k):
        pairs = []
        for i in range(fsdp):
            for j in range(tp):
                pairs.append((i * tp + j, (j * inner + i % inner) * tp + (i // inner + k) % tp))
        return lax.ppermute(x, ("fsdp", "tp"), pairs)

    xs = [spread(inputs, k) for k in range(1 if tp == 2 else 0, tp)]

    tick = pl.pallas_call(
        tick_kernel,
        out_shape=jax.ShapeDtypeStruct((8, 128), f32),
        out_specs=vmem(),
        cost_estimate=cost(8.0),
        name="tick",
    )()

    a_own, tick = lax.optimization_barrier((a_factor, tick))
    far = [over_fsdp(a_own, k) for k in range(1, inner)]

    def join(mine, other, bit):
        low = jnp.where(bit == 0, mine, other)
        high = jnp.where(bit == 0, other, mine)
        return jnp.concatenate([low, high], axis=1)

    def gather(x, axis, index, start, stop):
        size = {"fsdp": fsdp, "sub": sub}[axis]
        while start < stop:
            other = lax.ppermute(x, axis, [(i, i ^ start) for i in range(size)])
            x = join(x, other, (index // start) % 2)
            start = start * 2
        return x

    up = b_factor.transpose(0, 2, 1)
    direct = fsdp == 4 and inner == 2 and up.shape[1] % 16 == 0
    if direct:
        up = [up, over_fsdp(up, 1)]
    else:
        up = gather(gather(up[:, None], "fsdp", f, 1, fsdp), "sub", s, 1, sub)
        up = [up.reshape(2, sub, fsdp, -1, columns).swapaxes(1, 2).reshape(2, -1, columns)]

    count = group * tokens
    per_head = jax.ShapeDtypeStruct((heads, count, HD), f32)
    *state, up = pl.pallas_call(
        functools.partial(cache_kernel, group, len(up)),
        out_shape=[
            jax.ShapeDtypeStruct((heads, count, HD), bf16),
            per_head,
            per_head,
            per_head,
            jax.ShapeDtypeStruct((2, len(up) * up[0].shape[1], columns), bf16),
        ],
        in_specs=[smem(), vmem()] + [pl.BlockSpec(memory_space=pltpu.HBM)] * 2 + [vmem()] * len(up),
        out_specs=[vmem()] * 5,
        scratch_shapes=[
            pltpu.VMEM(queries.shape, bf16),
            pltpu.VMEM(kv_cache.shape, bf16),
            pltpu.SemaphoreType.DMA((3,)),
        ],
        compiler_params=params(40),
        cost_estimate=cost(C_CACHED),
        name="cached",
    )(lengths, tick, queries, kv_cache, *up)

    xs, near_a = lax.optimization_barrier((xs, up))
    if tp == 2:
        pairs = [(i * tp + i // inner, i * tp + 1 - i // inner) for i in range(fsdp)]
        xs = [inputs, xs[0], lax.ppermute(xs[0], ("fsdp", "tp"), pairs)]
    else:
        xs = jnp.stack(xs)
        xs = [lax.dynamic_index_in_dim(xs, (t - p - j) % tp, keepdims=False) for j in range(tp)]
    near = [(0, 0, a_factor)]
    up = [up, over_fsdp(up, inner)] if direct else [up]
    width = 2 * columns + 2 * ranks
    part, x, *x_sends = pl.pallas_call(
        functools.partial(early_kernel, tp, wide // 4, sizes, [(k, e) for k, e, _ in near]),
        out_shape=[
            jax.ShapeDtypeStruct((tp * tokens, width), f32),
            jax.ShapeDtypeStruct((tp * tokens, wide), bf16),
        ]
        + [jax.ShapeDtypeStruct((tp * tokens, a_factor.shape[2]), bf16)] * inner,
        in_specs=[pl.BlockSpec(memory_space=pltpu.HBM)] + [vmem()] * (len(xs) + len(near)),
        out_specs=[vmem()] * (2 + inner),
        scratch_shapes=[pltpu.VMEM((2, wide, columns), bf16), pltpu.SemaphoreType.DMA((8,))],
        compiler_params=params(50),
        cost_estimate=cost(C_EARLY),
        name="early",
    )(base, *xs, *[a for _, _, a in near])

    x_others = [over_sub(x, 1) for x in x_sends]
    far, part, up, x_others = lax.optimization_barrier((far, part, up, x_others))
    far_own, far_other = pl.pallas_call(
        functools.partial(far_kernel, sizes, inner),
        out_shape=[
            jax.ShapeDtypeStruct((tp * tokens, 2 * ranks), f32),
            jax.ShapeDtypeStruct((tp * tokens, 2 * ranks), bf16),
        ],
        in_specs=[vmem()] * (2 + 2 * inner),
        out_specs=[vmem()] * 2,
        compiler_params=params(),
        name="far",
    )(part, x, *x_others, a_factor, *far)
    parts = pl.pallas_call(
        functools.partial(late_kernel, columns),
        out_shape=[jax.ShapeDtypeStruct((tokens, width), f32 if j == 0 else bf16) for j in range(tp)],
        in_specs=[vmem()] * 3,
        out_specs=[vmem()] * tp,
        compiler_params=params(),
        name="late",
    )(part, far_own, over_sub(far_other, 1))

    parts, up = lax.optimization_barrier((parts, up))
    others = []
    for j in range(1, tp):
        pairs = [(i, (i + j * inner) % fsdp) for i in range(fsdp)]
        others.append(lax.ppermute(parts[j], "fsdp", pairs))

    if direct:
        rows_up = up[0].shape[1] * 2
        mine = pl.pallas_call(
            collect_kernel,
            out_shape=jax.ShapeDtypeStruct((2, rows_up, columns), bf16),
            in_specs=[vmem()] * 2,
            out_specs=vmem(),
            compiler_params=params(),
            name="collect",
        )(*up)
        up = [mine] + [over_sub(mine, e) for e in range(1, sub)]
        up = pl.pallas_call(
            functools.partial(order_kernel, fsdp, sub),
            out_shape=jax.ShapeDtypeStruct((2, sub * rows_up, columns), bf16),
            in_specs=[vmem()] * sub,
            out_specs=vmem(),
            compiler_params=params(),
        cost_estimate=cost(1.0),
            name="order",
        )(*up)
    else:
        up = up[0]

    own = pl.pallas_call(
        functools.partial(rank_kernel, columns),
        out_shape=jax.ShapeDtypeStruct((tokens, 2 * ranks), bf16),
        in_specs=[vmem()] * tp,
        out_specs=vmem(),
        compiler_params=params(),
        cost_estimate=cost(4.0),
        name="ranks",
    )(parts[0], *others)
    rank_parts = [own]
    for i in range(1, tp):
        rank_parts.append(lax.ppermute(own, "tp", [(j, (j + i) % tp) for j in range(tp)]))

    first = pl.pallas_call(
        functools.partial(first_kernel, tp),
        out_shape=jax.ShapeDtypeStruct((tokens, 2 * columns), f32),
        in_specs=[vmem()] * (tp + 2),
        out_specs=vmem(),
        compiler_params=params(),
        name="first",
    )(parts[0], *others, own, up)
    fresh, attended = pl.pallas_call(
        functools.partial(final_kernel, tp, steps, group),
        out_shape=(
            jax.ShapeDtypeStruct((2, row_count, steps, columns), bf16),
            jax.ShapeDtypeStruct(queries.shape, bf16),
        ),
        in_specs=[vmem()] * (tp + 5),
        out_specs=[vmem(), vmem()],
        compiler_params=params(),
        name="final",
    )(first, *rank_parts[1:], up, *state)
    return fresh, attended


def solution(mesh):
    sizes = tuple(mesh.shape[axis] for axis in ("fsdp", "tp", "sub"))
    return jax.shard_map(
        functools.partial(local, sizes),
        mesh=mesh,
        in_specs=(
            P(("groups", "fsdp", "sub"), None, "tp"),
            P(("groups", "fsdp", "sub"), None, "tp"),
            P(None, ("groups", "fsdp", "sub"), None, "tp"),
            P(("groups", "fsdp", "sub")),
            P(None, None, "tp"),
            P(None, "tp", ("fsdp", "sub")),
            P(None, "tp", ("fsdp", "sub")),
        ),
        out_specs=(
            P(None, ("groups", "fsdp", "sub"), None, "tp"),
            P(("groups", "fsdp", "sub"), None, "tp"),
        ),
        check_vma=False,
    )
```
